32 devices in a mesh: dp: 16 (over z, y, x), tensor: 2 (over core).
Axes of the slice: x: 2, y: 2, z: 4, core: 2. Of those that a mesh axis runs over, the one named last changes fastest.
Arguments:
- layer_in: bfloat16 [4096, 768], P(('dp', 'tensor')), may hold values from -6 to 6
- enc_states: bfloat16 [2048, 768], P(('dp', 'tensor')), may hold values from -6 to 6
- cotangent: bfloat16 [4096, 768], P(('dp', 'tensor')), may hold values from -6 to 6
- gain_self: float32 [768], replicated, may hold values from 0.25 to 1.75
- gain_cross: float32 [768], replicated, may hold values from 0.25 to 1.75
- gain_feed: float32 [768], replicated, may hold values from 0.25 to 1.75
- bias_table: float32 [32, 12], replicated, may hold values from -5 to 5
- self_query: bfloat16 [768, 768], P('dp', 'tensor'), may hold values from -0.0546875 to 0.0546875
- self_key: bfloat16 [768, 768], P('dp', 'tensor'), may hold values from -0.21875 to 0.21875
- self_value: bfloat16 [768, 768], P('dp', 'tensor'), may hold values from -0.21875 to 0.21875
- self_out: bfloat16 [768, 768], P('tensor', 'dp'), may hold values from -0.4375 to 0.4375
- cross_query: bfloat16 [768, 768], P('dp', 'tensor'), may hold values from -0.0546875 to 0.0546875
- cross_key: bfloat16 [768, 768], P('dp', 'tensor'), may hold values from -0.21875 to 0.21875
- cross_value: bfloat16 [768, 768], P('dp', 'tensor'), may hold values from -0.21875 to 0.21875
- cross_out: bfloat16 [768, 768], P('tensor', 'dp'), may hold values from -0.4375 to 0.4375
- gate_proj: bfloat16 [768, 2048], P('dp', 'tensor'), may hold values from -0.21875 to 0.21875
- up_proj: bfloat16 [768, 2048], P('dp', 'tensor'), may hold values from -0.21875 to 0.21875
- down_proj: bfloat16 [2048, 768], P('tensor', 'dp'), may hold values from -0.25 to 0.25
- dec_lengths: int32 [16], replicated, may hold values from 1 to 256, 3276 in all
- enc_lengths: int32 [16], replicated, may hold values from 1 to 128, 1280 in all
- seq_owner: int32 [16], replicated, may hold values from 0 to 15, each once
- bucket_table: int32 [256], replicated, may hold values from 0 to 31
Outputs:
- layer_out: bfloat16 [4096, 768], P(('dp', 'tensor'))
- grad_in: float32 [4096, 768], P(('dp', 'tensor'))
- grad_states: float32 [2048, 768], P(('dp', 'tensor'))
- grad_gain_self: float32 [768], replicated
- grad_gain_cross: float32 [768], replicated
- grad_gain_feed: float32 [768], replicated
- grad_table: float32 [32, 12], replicated
- grad_self_query: float32 [768, 768], P('dp', 'tensor')
- grad_self_key: float32 [768, 768], P('dp', 'tensor')
- grad_self_value: float32 [768, 768], P('dp', 'tensor')
- grad_self_out: float32 [768, 768], P('tensor', 'dp')
- grad_cross_query: float32 [768, 768], P('dp', 'tensor')
- grad_cross_key: float32 [768, 768], P('dp', 'tensor')
- grad_cross_value: float32 [768, 768], P('dp', 'tensor')
- grad_cross_out: float32 [768, 768], P('tensor', 'dp')
- grad_gate_proj: float32 [768, 2048], P('dp', 'tensor')
- grad_up_proj: float32 [768, 2048], P('dp', 'tensor')
- grad_down_proj: float32 [2048, 768], P('tensor', 'dp')
The draws below stay inside these ranges and needn't reach their ends.
Inputs may be any that keep to these rules, and one draw needn't show every extreme that they name: `dec_lengths`: one sequence has exactly 256 decoder tokens. `enc_lengths`: one sequence has exactly 128 encoder tokens. `seq_owner`: each sequence in exactly one slot.
All inputs are finite; a program needn't handle non-finite values.
Results may differ from the reference program's by a relative error of at most 0.039.
Values may be sent and summed in bfloat16 or wider, within the bound.
No kernel may reach another device: no remote copies, remote signals or barrier semaphores. Data moves between devices by JAX's collectives and lax.ppermute only.
A program may use at most 192 MiB of HBM per device.

```python
import math
import jax
import jax.numpy as jnp
import numpy as np
from jax import lax

D = 768
H = 12
DH = 64
FF = 2048
NB = 32
HD = 768
LEN = 256
ENC = 128
SEQS = 16
TOKENS = 4096
ENC_TOKENS = 2048
N_DP = 16


def plant(values, stream_key, smallest, top_value):
    shape = values.shape
    spot = [jax.random.randint(jax.random.fold_in(stream_key, axis), (), 0, shape[axis]) for axis in range(len(shape))]
    values = values.at[tuple(spot)].set(smallest)
    longest = shape.index(max(shape))
    spot[longest] = (spot[longest] + 1) % shape[longest]
    return values.at[tuple(spot)].set(top_value)


def strengthened(values, rng, source, target, blocks, factor):
    def block_of(axis_at):
        return (jnp.arange(values.shape[axis_at]) // (values.shape[axis_at] // blocks)).reshape((-1,) + (1,) * (values.ndim - 1 - axis_at))

    near = jax.random.permutation(rng, blocks)[block_of(target)]
    far = (block_of(target) + blocks // 2) % blocks
    return jnp.where((block_of(source) == near) | (block_of(source) == far), factor * values, values)


def block_levels(rng, extent, pieces, smallest, largest):
    factor_of = 1.0
    for dim, blocks in pieces:
        heights = jax.random.uniform(jax.random.fold_in(jax.random.fold_in(rng, 6), dim), (blocks,), jnp.float32, smallest / len(pieces), largest / len(pieces))
        factor_of = factor_of * jnp.repeat(jnp.exp(heights), extent[dim] // blocks).reshape((-1,) + (1,) * (len(extent) - 1 - dim))
    return factor_of


def profile(number_of, total, most, skew):
    loads = [(1 << 20) // math.isqrt(standing ** skew) + 1 for standing in range(2, number_of + 1)]
    surplus, given = total - most - (number_of - 1), [1] * (number_of - 1)
    while surplus > 0:
        candidates = [i for i in range(number_of - 1) if given[i] < most]
        mass, left = sum([loads[i] for i in candidates]), surplus
        for i in candidates:
            more = min(most - given[i], max(1, left * loads[i] // mass), surplus)
            given[i] = given[i] + more
            surplus = surplus - more
    return np.array([most] + given)


def uneven_parts(own_key, amount, total, bound, skew):
    if amount == 2:
        one = jax.random.randint(own_key, (), max(1, total - bound), min(bound, total - 1) + 1)
        return jnp.stack([one, total - one])
    tallies = jnp.asarray(profile(amount, total, bound, skew), jnp.int32)
    twos = (amount - 1) // 2
    source_of, receiver = tallies[1:1 + 2 * twos:2], tallies[2:2 + 2 * twos:2]
    slack = jnp.minimum(source_of - 1, bound - receiver)
    moved = jax.random.randint(jax.random.fold_in(own_key, 1), (twos,), 0, 1 << 20) % (slack + 1)
    tallies = tallies.at[1:1 + 2 * twos:2].set(source_of - moved).at[2:2 + 2 * twos:2].set(receiver + moved)
    return tallies[jax.random.permutation(jax.random.fold_in(own_key, 2), amount)]


def centred(rng, shape, spread, bound, split=(), held_as=jnp.bfloat16):
    factor_of = block_levels(rng, shape, split, -0.22, 0.18) if split else 1.0
    entries = jax.random.normal(rng, shape, jnp.float32) * spread * factor_of
    return jnp.minimum(jnp.maximum(entries, -bound), bound).astype(held_as)


def noise_with(stream_key, extent, spread, bound, pieces, heavy, held_as=jnp.bfloat16):
    entries = spread * jax.random.normal(stream_key, extent, jnp.float32)
    if pieces:
        entries = entries * block_levels(stream_key, extent, pieces, -0.22, 0.18)
    return jnp.clip(strengthened(entries, jax.random.fold_in(stream_key, 3), *heavy), -bound, bound).astype(held_as)


def setup_inputs(seed: int = 0) -> dict:
    key_of = jax.random.split(jax.random.key(seed), 23)
    layer_in = noise_with(key_of[0], (TOKENS, D), 1.0, 6.0, ((0, 32),), (0, 1, 32, 2.75))
    enc_states = noise_with(key_of[1], (ENC_TOKENS, D), 1.0, 6.0, ((0, 32),), (0, 1, 32, 2.75))
    cotangent = noise_with(key_of[2], (TOKENS, D), 1.0, 6.0, ((0, 32),), (0, 1, 32, 2.75))
    gain_self = jnp.clip(1.0 + 0.15 * jax.random.normal(key_of[3], (D,), jnp.float32), 0.25, 1.75)
    gain_cross = jnp.clip(1.0 + 0.15 * jax.random.normal(key_of[4], (D,), jnp.float32), 0.25, 1.75)
    gain_feed = jnp.clip(1.0 + 0.15 * jax.random.normal(key_of[5], (D,), jnp.float32), 0.25, 1.75)
    bias_table = centred(key_of[6], (NB, H), 1.0, 5.0, (), jnp.float32)
    self_query = centred(key_of[7], (D, HD), (16 * D) ** -0.5, 0.0546875, ((0, 16), (1, 2)))
    self_key = centred(key_of[8], (D, HD), D ** -0.5, 0.21875, ((0, 16), (1, 2)))
    self_value = centred(key_of[9], (D, HD), D ** -0.5, 0.21875, ((0, 16), (1, 2)))
    self_out = centred(key_of[10], (HD, D), (HD // 4) ** -0.5, 0.4375, ((0, 2), (1, 16)))
    cross_query = centred(key_of[11], (D, HD), (16 * D) ** -0.5, 0.0546875, ((0, 16), (1, 2)))
    cross_key = centred(key_of[12], (D, HD), D ** -0.5, 0.21875, ((0, 16), (1, 2)))
    cross_value = centred(key_of[13], (D, HD), D ** -0.5, 0.21875, ((0, 16), (1, 2)))
    cross_out = centred(key_of[14], (HD, D), (HD // 4) ** -0.5, 0.4375, ((0, 2), (1, 16)))
    gate_proj = centred(key_of[15], (D, FF), D ** -0.5, 0.21875, ((0, 16), (1, 2)))
    up_proj = centred(key_of[16], (D, FF), D ** -0.5, 0.21875, ((0, 16), (1, 2)))
    down_proj = centred(key_of[17], (FF, D), (FF // 4) ** -0.5, 0.25, ((0, 2), (1, 16)))
    dec_lengths = uneven_parts(key_of[18], SEQS, N_DP * LEN * 4 // 5, LEN, 1).astype(jnp.int32)
    enc_lengths = uneven_parts(key_of[19], SEQS, N_DP * ENC * 5 // 8, ENC, 1).astype(jnp.int32)
    seq_owner = jax.random.permutation(key_of[20], SEQS).astype(jnp.int32)
    bucket_table = plant(jax.random.randint(key_of[21], (LEN,), 0, NB), jax.random.fold_in(key_of[21], 1), 0, NB - 1).astype(jnp.int32)
    return dict(layer_in=layer_in, enc_states=enc_states, cotangent=cotangent, gain_self=gain_self, gain_cross=gain_cross, gain_feed=gain_feed, bias_table=bias_table, self_query=self_query, self_key=self_key, self_value=self_value, self_out=self_out, cross_query=cross_query, cross_key=cross_key, cross_value=cross_value, cross_out=cross_out, gate_proj=gate_proj, up_proj=up_proj, down_proj=down_proj, dec_lengths=dec_lengths, enc_lengths=enc_lengths, seq_owner=seq_owner, bucket_table=bucket_table)


@jax.custom_vjp
def low(v):
    return lax.optimization_barrier(v.astype(jnp.bfloat16)).astype(jnp.float32)

@jax.custom_vjp
def low_back(v):
    return v

def low_keep(v):
    return (low(v), None)

def low_pass(kept, grad):
    return (grad,)

def back_keep(v):
    return (v, None)

def back_low(kept, grad):
    return (low(grad),)
low.defvjp(low_keep, low_pass)
low_back.defvjp(back_keep, back_low)
EPSILON = 1e-06
NEGATIVE = -1e+30
HIGH = lax.Precision.HIGHEST

def matmul(left, right):
    return jnp.dot(left, right, precision=HIGH)

def norm_rows(values, gain):
    return values * lax.rsqrt(lax.optimization_barrier(jnp.mean(values * values, axis=-1, keepdims=True)) + EPSILON) * gain

def split_heads(matrix):
    return matrix.reshape(matrix.shape[0], -1, DH)

def attend(query, keys, values, extra, allowed):
    scores = jnp.einsum('qhd,khd->hqk', query, keys, precision=HIGH) + extra
    scores = low_back(scores)
    scores = jnp.where(allowed, scores, NEGATIVE)
    probs = jax.nn.softmax(scores, axis=-1)
    mixed = jnp.einsum('hqk,khd->qhd', low(probs), values, precision=HIGH)
    return low_back(low(mixed.reshape(mixed.shape[0], -1)))

def forward(layer_in, enc_states, gain_self, gain_cross, gain_feed, bias_table, self_query, self_key, self_value, self_out, cross_query, cross_key, cross_value, cross_out, gate_proj, up_proj, down_proj, slot_len, slot_enc, bucket_table):
    position = jnp.arange(LEN)
    distance = jnp.clip(position[:, None] - position[None, :], 0, LEN - 1)
    onehot = (bucket_table[:, None] == jnp.arange(NB)[None, :]).astype(bias_table.dtype)
    per_dist = matmul(onehot, bias_table)
    extra = jnp.transpose(per_dist[distance], (2, 0, 1))
    enc_position = jnp.arange(ENC)

    def one_slot(item):
        row_block, state_block, length, enc_len = item
        causal = ((position[None, :] <= position[:, None]) & (position[None, :] < length))[None]
        normed_self = low(norm_rows(row_block, gain_self))
        query = low_back(low(matmul(normed_self, self_query)))
        keys = low_back(low(matmul(normed_self, self_key)))
        values = low_back(low(matmul(normed_self, self_value)))
        mixed_self = attend(split_heads(query), split_heads(keys), split_heads(values), extra, causal)
        after_self = row_block + low_back(matmul(mixed_self, self_out))
        normed_cross = low(norm_rows(after_self, gain_cross))
        cross_q = low_back(low(matmul(normed_cross, cross_query)))
        cross_k = low_back(low(matmul(state_block, cross_key)))
        cross_v = low_back(low(matmul(state_block, cross_value)))
        allowed = (enc_position < enc_len)[None, None, :]
        mixed_cross = attend(split_heads(cross_q), split_heads(cross_k), split_heads(cross_v), 0.0, allowed)
        after_cross = after_self + low_back(matmul(mixed_cross, cross_out))
        normed_feed = low(norm_rows(after_cross, gain_feed))
        gate = low_back(matmul(normed_feed, gate_proj))
        upper = low_back(matmul(normed_feed, up_proj))
        hidden = low(jax.nn.gelu(gate, approximate=True) * upper)
        return after_cross + low_back(matmul(hidden, down_proj))
    slots = (layer_in.reshape(-1, LEN, D), enc_states.reshape(-1, ENC, D), slot_len, slot_enc)
    return lax.map(jax.checkpoint(one_slot), slots).reshape(-1, D)

def reference(layer_in, enc_states, cotangent, gain_self, gain_cross, gain_feed, bias_table, self_query, self_key, self_value, self_out, cross_query, cross_key, cross_value, cross_out, gate_proj, up_proj, down_proj, dec_lengths, enc_lengths, seq_owner, bucket_table):
    slot_len = dec_lengths[seq_owner]
    slot_enc = enc_lengths[seq_owner]
    floats = [array.astype(jnp.float32) for array in (layer_in, enc_states, gain_self, gain_cross, gain_feed, bias_table, self_query, self_key, self_value, self_out, cross_query, cross_key, cross_value, cross_out, gate_proj, up_proj, down_proj)]

    def apply(*params):
        return forward(*params, slot_len, slot_enc, bucket_table)
    result, pull = jax.vjp(apply, *floats)
    position = jnp.arange(LEN)
    valid = (position[None, :] < slot_len[:, None]).astype(jnp.float32).reshape(-1, 1)
    grads = pull(cotangent.astype(jnp.float32) * valid)
    return (result.astype(jnp.bfloat16), grads[0], grads[1], grads[2], grads[3], grads[4], grads[5], grads[6], grads[7], grads[8], grads[9], grads[10], grads[11], grads[12], grads[13], grads[14], grads[15], grads[16])
```

```python
import functools

import jax
import jax.numpy as jnp
from jax import lax
from jax.experimental import pallas as pl
from jax.experimental.pallas import tpu as pltpu
from jax.sharding import PartitionSpec as P

H = 12
DH = 64
NB = 32
LEN = 256
ENC = 128
EPSILON = 1e-06
NEGATIVE = -1e30
F32 = jnp.float32
BF16 = jnp.bfloat16
VMEM_LIMIT = 56 * 1024 * 1024


def product(left, right):
    return jnp.dot(left, right, preferred_element_type=F32)


def product_tn(left, right):
    return lax.dot_general(left, right, (((0,), (0,)), ((), ())), preferred_element_type=F32)


def product_nt(left, right):
    return lax.dot_general(left, right, (((1,), (1,)), ((), ())), preferred_element_type=F32)


def exact_nt(left, right):
    return lax.dot_general(
        left, right, (((1,), (1,)), ((), ())), preferred_element_type=F32, precision=lax.Precision.HIGHEST
    )


def inverse_rms(values):
    return lax.rsqrt(jnp.mean(values * values, axis=-1, keepdims=True) + EPSILON)


def norm_back(values, gain, upstream):
    inverse = inverse_rms(values)
    scaled = upstream * gain
    inner = jnp.mean(scaled * values, axis=-1, keepdims=True)
    grad_values = inverse * scaled - values * (inverse * inverse * inverse * inner)
    grad_gain = jnp.sum(upstream * values * inverse, axis=0, keepdims=True)
    return grad_values, grad_gain


def both_heads(pair):
    first = lax.broadcasted_iota(jnp.int32, pair.shape, 1) < DH
    zero = jnp.zeros_like(pair)
    return jnp.concatenate([jnp.where(first, pair, zero), jnp.where(first, zero, pair)], axis=0)


def join_heads(stacked):
    rows = stacked.shape[0] // 2
    first = lax.broadcasted_iota(jnp.int32, (rows, stacked.shape[1]), 1) < DH
    return jnp.where(first, stacked[:rows], stacked[rows:])


def softmax(scores):
    expo = jnp.exp(scores - jnp.max(scores, axis=-1, keepdims=True))
    return expo * (1.0 / jnp.sum(expo, axis=-1, keepdims=True))


def attend_back(query, keys, values, probs, upstream):
    upper = both_heads(upstream)
    grad_probs = product_nt(upper, values)
    inner = jnp.sum(probs * grad_probs, axis=-1, keepdims=True)
    grad_scores = (probs * (grad_probs - inner)).astype(BF16)
    grad_query = join_heads(product(grad_scores, keys)).astype(BF16)
    grad_keys = product_tn(grad_scores, both_heads(query)).astype(BF16)
    grad_values = product_tn(probs.astype(BF16), upper).astype(BF16)
    return grad_query, grad_keys, grad_values, grad_scores


def bucket_onehot(buckets):
    return (lax.broadcasted_iota(jnp.int32, (NB, LEN), 0) == buckets).astype(F32)


def reversal():
    shape = (LEN, LEN)
    return (
        lax.broadcasted_iota(jnp.int32, shape, 0) + lax.broadcasted_iota(jnp.int32, shape, 1) == LEN - 1
    ).astype(BF16)


class Plan:
    def __init__(self, mesh, rows):
        self.size = mesh.shape["dp"]
        self.rows = rows
        self.staged = self.size == 16 and rows % 16 == 0
        self.pieces = 8 if self.staged else 1

    def place(self):
        index = lax.axis_index("dp")
        return index >> 2, (index >> 1) & 1, index & 1

    def spans(self, forward):
        if not self.staged:
            return [(0, 0, 0, self.size * self.rows, None)]
        z, y, x = self.place()
        sign = -1 if forward else 1
        result = []
        for way in range(4):
            dy, dx = way >> 1, way & 1
            for step in range(4):
                source = ((z + sign * step) & 3) * 4 + (y ^ dy) * 2 + (x ^ dx)
                first = pl.multiple_of(source * self.rows, 16)
                for half in range(2):
                    result.append((2 * way + half, step * self.rows, first, self.rows, half))
        return result

    def copies(self, pieces, whole, sems, forward):
        width = whole.shape[1] // 2
        result = []
        for number, (piece, row, first, rows, half) in enumerate(self.spans(forward)):
            columns = pl.ds(0, 2 * width) if half is None else pl.ds(half * width, width)
            part = pieces[piece].at[pl.ds(row, rows), :]
            block = whole.at[pl.ds(first, rows), columns]
            ends = (part, block) if forward else (block, part)
            result.append(pltpu.make_async_copy(*ends, sems.at[number]))
        return result

    def n_copies(self):
        return 32 if self.staged else 1

    def piece_shapes(self, width):
        if self.staged:
            return [jax.ShapeDtypeStruct((4 * self.rows, width // 2), BF16)] * 8
        return [jax.ShapeDtypeStruct((self.size * self.rows, width), BF16)]


def swap(block, axis_bit, size):
    return lax.ppermute(block, "dp", [(i, i ^ axis_bit) for i in range(size)])


def shift_z(block, step):
    return lax.ppermute(block, "dp", [(i, (((i >> 2) + step) & 3) * 4 + (i & 3)) for i in range(16)])


def gather(plan, block):
    if not plan.staged:
        return [lax.all_gather(block, "dp", axis=0, tiled=True)]
    column = jnp.concatenate([block] + [shift_z(block, step) for step in (1, 2, 3)], axis=0)
    half = block.shape[1] // 2
    one, two = column[:, :half], column[:, half:]
    one_x = swap(one, 1, 16)
    two_y = swap(two, 2, 16)
    one_y = swap(one, 2, 16)
    two_x = swap(two, 1, 16)
    one_d = swap(one_x, 2, 16)
    two_d = swap(two_y, 1, 16)
    return [one, two, one_x, two_x, one_y, two_y, one_d, two_d]


def scatter_sum(plan, pieces):
    if not plan.staged:
        return [lax.psum_scatter(pieces[0].astype(F32), "dp", scatter_dimension=0, tiled=True)]
    one, two, one_x, two_x, one_y, two_y, one_d, two_d = pieces
    wide = lambda value: value.astype(F32)
    got_d1 = swap(one_d, 2, 16)
    got_d2 = swap(two_d, 1, 16)
    got_y1 = swap(one_y, 2, 16)
    got_x2 = swap(two_x, 1, 16)
    got_x1 = swap((wide(one_x) + wide(got_d1)).astype(BF16), 1, 16)
    got_y2 = swap((wide(two_y) + wide(got_d2)).astype(BF16), 2, 16)
    total = jnp.concatenate(
        [
            (wide(one) + wide(got_y1) + wide(got_x1)).astype(BF16),
            (wide(two) + wide(got_x2) + wide(got_y2)).astype(BF16),
        ],
        axis=1,
    )
    rows = plan.rows
    return [total[:rows]] + [shift_z(total[step * rows : (step + 1) * rows], step) for step in (1, 2, 3)]


def other_core(block):
    return lax.ppermute(block, "tensor", [(0, 1), (1, 0)])


def sum_everywhere(plan, block):
    if plan.size & (plan.size - 1):
        return lax.psum(block, ("dp", "tensor"))
    total = block + other_core(block)
    bit = 1
    while bit < plan.size:
        total = total + swap(total, bit, plan.size)
        bit *= 2
    return total


VM = pl.BlockSpec(memory_space=pltpu.VMEM)
SM = pl.BlockSpec(memory_space=pltpu.SMEM)
ANY = pl.BlockSpec(memory_space=pl.ANY)


def call(body, name, inputs, specs, outputs, out_specs, scratch, flops):
    nbytes = sum(a.size * a.dtype.itemsize for a in inputs) + sum(
        a.size * jnp.dtype(a.dtype).itemsize for a in outputs
    )
    return pl.pallas_call(
        body,
        name=name,
        out_shape=outputs,
        in_specs=specs,
        out_specs=out_specs,
        scratch_shapes=scratch,
        compiler_params=pltpu.CompilerParams(vmem_limit_bytes=VMEM_LIMIT),
        cost_estimate=pl.CostEstimate(flops=flops, bytes_accessed=nbytes, transcendentals=0),
    )(*inputs)


def shape(*dims, dtype=F32):
    return jax.ShapeDtypeStruct(dims, dtype)


def rows_of(mine, other, core):
    first = jnp.where(core == 0, mine, other)
    second = jnp.where(core == 0, other, mine)
    return jnp.concatenate([first, second], axis=0)


def wide_sum(mine, other):
    return mine[...].astype(F32) + other[...].astype(F32)


def turned(matrix):
    n = matrix.shape[0]
    eye = (
        lax.broadcasted_iota(jnp.int32, (n, n), 0) == lax.broadcasted_iota(jnp.int32, (n, n), 1)
    ).astype(BF16)
    return product_tn(matrix, eye).astype(BF16)


def pack_attention(plan, query, key, value, out):
    rows, width = query.shape
    if rows % 16:
        return jnp.concatenate([query, key, value, out.T], axis=1)

    def body(q, k, v, o, packed):
        packed[:, :width] = q[...]
        packed[:, width : 2 * width] = k[...]
        packed[:, 2 * width : 3 * width] = v[...]
        packed[:, 3 * width :] = turned(o[...])

    return call(
        body, "pack", [query, key, value, out], [VM] * 4, shape(rows, 4 * width, dtype=BF16), VM, [], 1 << 20
    ) if False else pl.pallas_call(
        body,
        name="pack_attention",
        out_shape=shape(rows, 4 * width, dtype=BF16),
        in_specs=[VM] * 4,
        out_specs=VM,
        compiler_params=pltpu.CompilerParams(vmem_limit_bytes=VMEM_LIMIT),
    )(query, key, value, out)


def pack_feed(plan, gate, up, down):
    rows, width = gate.shape
    half = width // 2
    if rows % 16:
        turned_down = down.T
        return [
            jnp.concatenate([m[:, i * half : (i + 1) * half] for m in (gate, up, turned_down)], axis=1)
            for i in range(2)
        ]

    def body(g, u, d, *packed):
        for i in range(2):
            units = slice(i * half, (i + 1) * half)
            packed[i][:, :half] = g[:, units]
            packed[i][:, half : 2 * half] = u[:, units]
            packed[i][:, 2 * half :] = turned(d[units, :])

    return pl.pallas_call(
        body,
        name="pack_feed",
        out_shape=[shape(rows, 3 * half, dtype=BF16)] * 2,
        in_specs=[VM] * 3,
        out_specs=[VM] * 2,
        compiler_params=pltpu.CompilerParams(vmem_limit_bytes=VMEM_LIMIT),
    )(gate, up, down)


def bring(plan, pieces, whole, sems):
    copies = plan.copies(pieces, whole, sems, True)
    for copy in copies:
        copy.start()
    return copies


def finish(copies):
    for copy in copies:
        copy.wait()


def hand_out(plan, pieces, whole, sems):
    copies = plan.copies(pieces, whole, sems, False)
    for copy in copies:
        copy.start()
    finish(copies)


def self_forward(plan, pieces, x_mine, x_other, gain, table, buckets, dec_lengths, owner):
    n = plan.pieces
    d = x_mine.shape[1]
    width = sum(p.shape[1] for p in pieces[:2]) // 4 if plan.staged else pieces[0].shape[1] // 4
    pairs = width // (2 * DH)

    def body(*refs):
        weights = refs[:n]
        xm, xo, g, tab, buck, lens, own = refs[n : n + 7]
        part, normed_ref, qkv, probs_ref, mixed_ref, whole, sems = refs[n + 7 :]
        copies = bring(plan, weights, whole, sems)
        core = lax.axis_index("tensor")
        length = lens[own[lax.axis_index("dp")]]
        x = rows_of(xm[...], xo[...], core).astype(F32)
        normed = (x * inverse_rms(x) * g[...]).astype(BF16)
        normed_ref[...] = normed
        distances = lax.dot_general(
            tab[...], bucket_onehot(buck[...]), (((1,), (0,)), ((), ())),
            preferred_element_type=F32, precision=lax.Precision.HIGHEST,
        )
        heads = 2 * pairs
        mine = distances[:heads]
        for other in range(1, H // heads):
            mine = jnp.where(core == other, distances[other * heads : (other + 1) * heads], mine)
        row = lax.broadcasted_iota(jnp.int32, (2 * LEN, LEN), 0) & (LEN - 1)
        key = lax.broadcasted_iota(jnp.int32, (2 * LEN, LEN), 1)
        allowed = (key <= row) & (key < length)
        finish(copies)
        qkv[...] = product(normed, whole[:, : 3 * width]).astype(BF16)
        for pair in range(pairs):
            lanes = slice(pair * 128, (pair + 1) * 128)
            query = qkv[:, lanes]
            keys = qkv[:, width + pair * 128 : width + (pair + 1) * 128]
            values = qkv[:, 2 * width + pair * 128 : 2 * width + (pair + 1) * 128]
            extra = jnp.concatenate(
                [
                    pltpu.roll(
                        jnp.broadcast_to(mine[h : h + 1], (LEN, LEN)), 0, 1, stride=1, stride_axis=0
                    )
                    for h in (2 * pair, 2 * pair + 1)
                ],
                axis=0,
            )
            scores = product_nt(both_heads(query), keys) + extra
            probs = softmax(jnp.where(allowed, scores, NEGATIVE))
            probs_ref[pl.ds(pair * 2 * LEN, 2 * LEN), :] = probs
            mixed_ref[:, lanes] = join_heads(product(probs.astype(BF16), values)).astype(BF16)
        part[...] = product_nt(mixed_ref[...], whole[:, 3 * width :]).astype(BF16)

    outputs = [
        shape(LEN, d, dtype=BF16),
        shape(LEN, d, dtype=BF16),
        shape(LEN, 3 * width, dtype=BF16),
        shape(pairs * 2 * LEN, LEN),
        shape(LEN, width, dtype=BF16),
    ]
    return call(
        body,
        "self_forward",
        [*pieces, x_mine, x_other, gain, table, buckets, dec_lengths, owner],
        [ANY] * n + [VM] * 5 + [SM] * 2,
        outputs,
        [VM] * 5,
        [pltpu.VMEM((d, 4 * width), BF16), pltpu.SemaphoreType.DMA((plan.n_copies(),))],
        2 * LEN * d * 4 * width + 8 * LEN * LEN * width,
    )


def cross_forward(plan, pieces, x_mine, x_other, part_mine, part_other, gain, e_mine, e_other, enc_lengths, owner):
    n = plan.pieces
    d = x_mine.shape[1]
    width = sum(p.shape[1] for p in pieces[:2]) // 4 if plan.staged else pieces[0].shape[1] // 4
    pairs = width // (2 * DH)

    def body(*refs):
        weights = refs[:n]
        xm, xo, pm, po, g, em, eo, lens, own = refs[n : n + 9]
        part, after_ref, normed_ref, q_ref, kv, probs_ref, mixed_ref, whole, sems = refs[n + 9 :]
        copies = bring(plan, weights, whole, sems)
        core = lax.axis_index("tensor")
        length = lens[own[lax.axis_index("dp")]]
        after = rows_of(xm[...], xo[...], core).astype(F32) + wide_sum(pm, po)
        after_ref[...] = after
        normed = (after * inverse_rms(after) * g[...]).astype(BF16)
        normed_ref[...] = normed
        allowed = lax.broadcasted_iota(jnp.int32, (2 * LEN, ENC), 1) < length
        finish(copies)
        kv[...] = product(rows_of(em[...], eo[...], core), whole[:, width : 3 * width]).astype(BF16)
        q_ref[...] = product(normed, whole[:, :width]).astype(BF16)
        for pair in range(pairs):
            lanes = slice(pair * 128, (pair + 1) * 128)
            keys = kv[:, lanes]
            values = kv[:, width + pair * 128 : width + (pair + 1) * 128]
            scores = product_nt(both_heads(q_ref[:, lanes]), keys)
            probs = softmax(jnp.where(allowed, scores, NEGATIVE))
            probs_ref[pl.ds(pair * 2 * LEN, 2 * LEN), :] = probs
            mixed_ref[:, lanes] = join_heads(product(probs.astype(BF16), values)).astype(BF16)
        part[...] = product_nt(mixed_ref[...], whole[:, 3 * width :]).astype(BF16)

    outputs = [
        shape(LEN, d, dtype=BF16),
        shape(LEN, d),
        shape(LEN, d, dtype=BF16),
        shape(LEN, width, dtype=BF16),
        shape(ENC, 2 * width, dtype=BF16),
        shape(pairs * 2 * LEN, ENC),
        shape(LEN, width, dtype=BF16),
    ]
    return call(
        body,
        "cross_forward",
        [*pieces, x_mine, x_other, part_mine, part_other, gain, e_mine, e_other, enc_lengths, owner],
        [ANY] * n + [VM] * 7 + [SM] * 2,
        outputs,
        [VM] * 7,
        [pltpu.VMEM((d, 4 * width), BF16), pltpu.SemaphoreType.DMA((plan.n_copies(),))],
        2 * LEN * d * 3 * width + 4 * LEN * ENC * width,
    )


GELU_C = 0.7978845608028654


def feed_units(normed, top, whole, grads, units):
    gate = product(normed, whole[:, :units])
    upper = product(normed, whole[:, units : 2 * units])
    square = gate * gate
    tanh = jnp.tanh(GELU_C * gate * (1.0 + 0.044715 * square))
    half = 0.5 * (1.0 + tanh)
    gelu = gate * half
    slope = half + 0.5 * gate * (1.0 - tanh * tanh) * (GELU_C * (1.0 + 3 * 0.044715 * square))
    hidden = (gelu * upper).astype(BF16)
    grad_hidden = product(top, whole[:, 2 * units :])
    grad_gate = (grad_hidden * upper * slope).astype(BF16)
    grad_up = (grad_hidden * gelu).astype(BF16)
    out = product_nt(hidden, whole[:, 2 * units :])
    back = product_nt(grad_gate, whole[:, :units]) + product_nt(grad_up, whole[:, units : 2 * units])
    grads[:, :units] = product_tn(normed, grad_gate).astype(BF16)
    grads[:, units : 2 * units] = product_tn(normed, grad_up).astype(BF16)
    grads[:, 2 * units :] = product_tn(top, hidden).astype(BF16)
    return out, back


def feed_first(plan, pieces, after_self, part_mine, part_other, gain, c_mine, c_other, dec_lengths, owner):
    n = plan.pieces
    d = after_self.shape[1]
    total = pieces[0].shape[1] * (2 if plan.staged else 1)
    units = total // 3

    def body(*refs):
        weights = refs[:n]
        a_ref, pm, po, g, cm, co, lens, own = refs[n : n + 8]
        after_ref, normed_ref, top_ref, out_ref, back_ref = refs[n + 8 : n + 13]
        grads_out = refs[n + 13 : 2 * n + 13]
        whole, grads, sems = refs[2 * n + 13 :]
        copies = bring(plan, weights, whole, sems)
        core = lax.axis_index("tensor")
        length = lens[own[lax.axis_index("dp")]]
        after = a_ref[...] + wide_sum(pm, po)
        after_ref[...] = after
        normed = (after * inverse_rms(after) * g[...]).astype(BF16)
        normed_ref[...] = normed
        cot = rows_of(cm[...], co[...], core)
        valid = lax.broadcasted_iota(jnp.int32, cot.shape, 0) < length
        top = jnp.where(valid, cot.astype(F32), 0.0).astype(BF16)
        top_ref[...] = top
        finish(copies)
        out_ref[...], back_ref[...] = feed_units(normed, top, whole, grads, units)
        hand_out(plan, grads_out, grads, sems)

    outputs = [
        shape(LEN, d),
        shape(LEN, d, dtype=BF16),
        shape(LEN, d, dtype=BF16),
        shape(LEN, d),
        shape(LEN, d),
        *plan.piece_shapes(total),
    ]
    return call(
        body,
        "feed_first",
        [*pieces, after_self, part_mine, part_other, gain, c_mine, c_other, dec_lengths, owner],
        [ANY] * n + [VM] * 6 + [SM] * 2,
        outputs,
        [VM] * 5 + [ANY] * n,
        [
            pltpu.VMEM((d, total), BF16),
            pltpu.VMEM((d, total), BF16),
            pltpu.SemaphoreType.DMA((plan.n_copies(),)),
        ],
        2 * LEN * d * 9 * units,
    )


def feed_second(plan, pieces, normed, top, out, back):
    n = plan.pieces
    d = normed.shape[1]
    total = pieces[0].shape[1] * (2 if plan.staged else 1)
    units = total // 3

    def body(*refs):
        weights = refs[:n]
        normed_ref, top_ref, out_ref, back_ref = refs[n : n + 4]
        sums = refs[n + 4]
        grads_out = refs[n + 5 : 2 * n + 5]
        whole, grads, sems = refs[2 * n + 5 :]
        copies = bring(plan, weights, whole, sems)
        finish(copies)
        more_out, more_back = feed_units(normed_ref[...], top_ref[...], whole, grads, units)
        sums[:LEN, :] = (back_ref[...] + more_back).astype(BF16)
        sums[LEN:, :] = (out_ref[...] + more_out).astype(BF16)
        hand_out(plan, grads_out, grads, sems)

    return call(
        body,
        "feed_second",
        [*pieces, normed, top, out, back],
        [ANY] * n + [VM] * 4,
        [shape(2 * LEN, d, dtype=BF16), *plan.piece_shapes(total)],
        [VM] + [ANY] * n,
        [
            pltpu.VMEM((d, total), BF16),
            pltpu.VMEM((d, total), BF16),
            pltpu.SemaphoreType.DMA((plan.n_copies(),)),
        ],
        2 * LEN * d * 9 * units,
    )


def cross_backward(
    plan, pieces, after_cross, top, sums_mine, sums_other, gain, normed, query, kv, probs, mixed, e_mine, e_other
):
    n = plan.pieces
    d = normed.shape[1]
    width = query.shape[1]
    pairs = width // (2 * DH)
    half_rows = LEN // 2

    def body(*refs):
        weights = refs[:n]
        after, top_ref, sm, so, g, normed_ref, q_ref, kv_ref, probs_ref, mixed_ref, em, eo = refs[n : n + 12]
        total_ref, sums, layer_out, grad_gain = refs[n + 12 : n + 16]
        grads_out = refs[n + 16 : 2 * n + 16]
        whole, grads, grad_q, grad_kv, sems = refs[2 * n + 16 :]
        copies = bring(plan, weights, whole, sems)
        core = lax.axis_index("tensor")
        back, gain_row = norm_back(after[...], g[...], wide_sum(sm.at[:LEN], so.at[:LEN]))
        grad_gain[...] = gain_row
        total = top_ref[...].astype(F32) + back
        total_ref[...] = total
        upstream = total.astype(BF16)
        first = pl.multiple_of(core * half_rows, half_rows)
        tail = pl.ds(pl.multiple_of(LEN + core * half_rows, half_rows), half_rows)
        layer_out[...] = (
            after[pl.ds(first, half_rows), :] + sm[tail, :].astype(F32) + so[tail, :].astype(F32)
        ).astype(BF16)
        states = rows_of(em[...], eo[...], core)
        finish(copies)
        grad_mixed = product(upstream, whole[:, 3 * width :]).astype(BF16)
        for pair in range(pairs):
            lanes = slice(pair * 128, (pair + 1) * 128)
            lanes_v = slice(width + pair * 128, width + (pair + 1) * 128)
            gq, gk, gv, _ = attend_back(
                q_ref[:, lanes],
                kv_ref[:, lanes],
                kv_ref[:, lanes_v],
                probs_ref[pl.ds(pair * 2 * LEN, 2 * LEN), :],
                grad_mixed[:, lanes],
            )
            grad_q[:, lanes] = gq
            grad_kv[:, lanes] = gk
            grad_kv[:, lanes_v] = gv
        sums[:LEN, :] = product_nt(grad_q[...], whole[:, :width]).astype(BF16)
        sums[LEN:, :] = product_nt(grad_kv[...], whole[:, width : 3 * width]).astype(BF16)
        grads[:, :width] = product_tn(normed_ref[...], grad_q[...]).astype(BF16)
        grads[:, width : 3 * width] = product_tn(states, grad_kv[...]).astype(BF16)
        grads[:, 3 * width :] = product_tn(upstream, mixed_ref[...]).astype(BF16)
        hand_out(plan, grads_out, grads, sems)

    return call(
        body,
        "cross_backward",
        [*pieces, after_cross, top, sums_mine, sums_other, gain, normed, query, kv, probs, mixed, e_mine, e_other],
        [ANY] * n + [VM] * 12,
        [
            shape(LEN, d),
            shape(LEN + ENC, d, dtype=BF16),
            shape(half_rows, d, dtype=BF16),
            shape(1, d),
            *plan.piece_shapes(4 * width),
        ],
        [VM] * 4 + [ANY] * n,
        [
            pltpu.VMEM((d, 4 * width), BF16),
            pltpu.VMEM((d, 4 * width), BF16),
            pltpu.VMEM((LEN, width), BF16),
            pltpu.VMEM((ENC, 2 * width), BF16),
            pltpu.SemaphoreType.DMA((plan.n_copies(),)),
        ],
        2 * LEN * d * 6 * width + 10 * LEN * ENC * width,
    )


def self_backward(
    plan, pieces, total_cross, after_self, sums_mine, sums_other, gain, normed, qkv, probs, mixed, buckets
):
    n = plan.pieces
    d = normed.shape[1]
    width = mixed.shape[1]
    pairs = width // (2 * DH)
    half_enc = ENC // 2

    def body(*refs):
        weights = refs[:n]
        tc, after, sm, so, g, normed_ref, qkv_ref, probs_ref, mixed_ref, buck = refs[n : n + 10]
        total_ref, sums, states_out, grad_gain, table_out = refs[n + 10 : n + 15]
        grads_out = refs[n + 15 : 2 * n + 15]
        whole, grads, grad_qkv, sems = refs[2 * n + 15 :]
        copies = bring(plan, weights, whole, sems)
        core = lax.axis_index("tensor")
        back, gain_row = norm_back(after[...], g[...], wide_sum(sm.at[:LEN], so.at[:LEN]))
        grad_gain[...] = gain_row
        total = tc[...] + back
        total_ref[...] = total
        upstream = total.astype(BF16)
        tail = pl.ds(pl.multiple_of(LEN + core * half_enc, half_enc), half_enc)
        states_out[...] = sm[tail, :].astype(F32) + so[tail, :].astype(F32)
        finish(copies)
        grad_mixed = product(upstream, whole[:, 3 * width :]).astype(BF16)
        backwards = reversal()
        per_distance = []
        for pair in range(pairs):
            lanes = slice(pair * 128, (pair + 1) * 128)
            lanes_k = slice(width + pair * 128, width + (pair + 1) * 128)
            lanes_v = slice(2 * width + pair * 128, 2 * width + (pair + 1) * 128)
            gq, gk, gv, gs = attend_back(
                qkv_ref[:, lanes],
                qkv_ref[:, lanes_k],
                qkv_ref[:, lanes_v],
                probs_ref[pl.ds(pair * 2 * LEN, 2 * LEN), :],
                grad_mixed[:, lanes],
            )
            grad_qkv[:, lanes] = gq
            grad_qkv[:, lanes_k] = gk
            grad_qkv[:, lanes_v] = gv
            turned_scores = product(gs, backwards)
            for h in range(2):
                rolled = pltpu.roll(
                    turned_scores[h * LEN : (h + 1) * LEN], 0, 1, stride=1, stride_axis=0
                )
                per_distance.append(jnp.sum(rolled, axis=0, keepdims=True))
        sums[...] = product_nt(grad_qkv[...], whole[:, : 3 * width]).astype(BF16)
        per_distance += [jnp.zeros_like(per_distance[0])] * (8 - len(per_distance))
        table_out[...] = exact_nt(jnp.concatenate(per_distance, axis=0), bucket_onehot(buck[...]))
        grads[:, : 3 * width] = product_tn(normed_ref[...], grad_qkv[...]).astype(BF16)
        grads[:, 3 * width :] = product_tn(upstream, mixed_ref[...]).astype(BF16)
        hand_out(plan, grads_out, grads, sems)

    return call(
        body,
        "self_backward",
        [*pieces, total_cross, after_self, sums_mine, sums_other, gain, normed, qkv, probs, mixed, buckets],
        [ANY] * n + [VM] * 10,
        [
            shape(LEN, d),
            shape(LEN, d, dtype=BF16),
            shape(half_enc, d),
            shape(1, d),
            shape(8, NB),
            *plan.piece_shapes(4 * width),
        ],
        [VM] * 5 + [ANY] * n,
        [
            pltpu.VMEM((d, 4 * width), BF16),
            pltpu.VMEM((d, 4 * width), BF16),
            pltpu.VMEM((LEN, 3 * width), BF16),
            pltpu.SemaphoreType.DMA((plan.n_copies(),)),
        ],
        2 * LEN * d * 8 * width + 14 * LEN * LEN * width,
    )


def last_norm(total_self, x_mine, x_other, sums_mine, sums_other, gain, gain_cross_row, gain_feed_row, table):
    d = total_self.shape[1]
    half_rows = LEN // 2
    heads = H // 2

    def body(total, xm, xo, sm, so, g, ggc, ggf, tab, grad_in, small):
        core = lax.axis_index("tensor")
        x = rows_of(xm[...], xo[...], core).astype(F32)
        upstream = wide_sum(sm, so)
        back, gain_row = norm_back(x, g[...], upstream)
        whole = total[...] + back
        grad_in[...] = jnp.where(core == 0, whole[:half_rows], whole[half_rows:])
        small[...] = jnp.zeros_like(small)
        once = (core == 0).astype(F32)
        small[0:1, :] = gain_row * once
        small[1:2, :] = ggc[...] * once
        small[2:3, :] = ggf[...] * once
        small[8 : 8 + heads, :NB] = tab[:heads, :] * once
        small[16 : 16 + heads, :NB] = tab[:heads, :] * (1.0 - once)

    return call(
        body,
        "last_norm",
        [total_self, x_mine, x_other, sums_mine, sums_other, gain, gain_cross_row, gain_feed_row, table],
        [VM] * 9,
        [shape(half_rows, d), shape(24, d)],
        [VM] * 2,
        [],
        1 << 24,
    )


def shards(
    mesh,
    layer_in,
    enc_states,
    cotangent,
    gain_self,
    gain_cross,
    gain_feed,
    bias_table,
    self_query,
    self_key,
    self_value,
    self_out,
    cross_query,
    cross_key,
    cross_value,
    cross_out,
    gate_proj,
    up_proj,
    down_proj,
    dec_lengths,
    enc_lengths,
    seq_owner,
    bucket_table,
):
    plan = Plan(mesh, self_query.shape[0])
    d = layer_in.shape[1]
    g_self, g_cross, g_feed = (g.reshape(1, d) for g in (gain_self, gain_cross, gain_feed))
    w_self = gather(plan, pack_attention(plan, self_query, self_key, self_value, self_out))
    w_cross = gather(plan, pack_attention(plan, cross_query, cross_key, cross_value, cross_out))
    w_feed = [gather(plan, block) for block in pack_feed(plan, gate_proj, up_proj, down_proj)]
    x_other = other_core(layer_in)
    e_other = other_core(enc_states)
    c_other = other_core(cotangent)
    buckets = jnp.concatenate([bucket_table[:1], bucket_table[:0:-1]]).reshape(1, LEN)
    buckets_up = jnp.concatenate([bucket_table[1:], bucket_table[:1]]).reshape(1, LEN)

    part, normed_s, qkv, probs_s, mixed_s = self_forward(
        plan, w_self, layer_in, x_other, g_self, bias_table.T, buckets, dec_lengths, seq_owner
    )
    part, after_self, normed_c, cq, ckv, probs_c, mixed_c = cross_forward(
        plan, w_cross, layer_in, x_other, part, other_core(part), g_cross, enc_states, e_other, enc_lengths, seq_owner
    )
    after_cross, normed_f, top, out, back, *grads_f1 = feed_first(
        plan, w_feed[0], after_self, part, other_core(part), g_feed, cotangent, c_other, dec_lengths, seq_owner
    )
    terms_f1 = scatter_sum(plan, grads_f1)
    sums, *grads_f2 = feed_second(plan, w_feed[1], normed_f, top, out, back)
    terms_f2 = scatter_sum(plan, grads_f2)
    total_cross, sums, layer_out, gain_feed_row, *grads_c = cross_backward(
        plan, w_cross, after_cross, top, sums, other_core(sums), g_feed, normed_c, cq, ckv, probs_c, mixed_c,
        enc_states, e_other,
    )
    terms_c = scatter_sum(plan, grads_c)
    total_self, sums, grad_states, gain_cross_row, table, *grads_s = self_backward(
        plan, w_self, total_cross, after_self, sums, other_core(sums), g_cross, normed_s, qkv, probs_s, mixed_s,
        buckets_up,
    )
    terms_s = scatter_sum(plan, grads_s)
    grad_in, small = last_norm(
        total_self, layer_in, x_other, sums, other_core(sums), g_self, gain_cross_row, gain_feed_row, table
    )
    small = sum_everywhere(plan, small)
    heads = H // 2
    table_grad = jnp.concatenate([small[8 : 8 + heads, :NB], small[16 : 16 + heads, :NB]], axis=0).T

    def summed(terms):
        return functools.reduce(lambda a, b: a + b, [t.astype(F32) for t in terms])

    width = self_query.shape[1]
    grad_s, grad_c = summed(terms_s), summed(terms_c)
    grad_f = [summed(terms_f1), summed(terms_f2)]
    units = grad_f[0].shape[1] // 3

    def columns(block, number, size):
        return block[:, number * size : (number + 1) * size]

    def feed(number):
        return jnp.concatenate([columns(g, number, units) for g in grad_f], axis=1)

    return (
        layer_out,
        grad_in,
        grad_states,
        small[0],
        small[1],
        small[2],
        table_grad,
        columns(grad_s, 0, width),
        columns(grad_s, 1, width),
        columns(grad_s, 2, width),
        columns(grad_s, 3, width).T,
        columns(grad_c, 0, width),
        columns(grad_c, 1, width),
        columns(grad_c, 2, width),
        columns(grad_c, 3, width).T,
        feed(0),
        feed(1),
        feed(2).T,
    )


def solution(mesh):
    rows = P(("dp", "tensor"), None)
    into, out = P("dp", "tensor"), P("tensor", "dp")
    weights = (into, into, into, out, into, into, into, out, into, into, out)
    in_specs = (rows, rows, rows, P(), P(), P(), P(), *weights, P(), P(), P(), P())
    out_specs = (rows, rows, rows, P(), P(), P(), P(), *weights)
    return jax.shard_map(
        functools.partial(shards, mesh), mesh=mesh, in_specs=in_specs, out_specs=out_specs, check_vma=False
    )
```

```python
import functools

import jax
import jax.numpy as jnp
from jax import lax
from jax.experimental import pallas as pl
from jax.experimental.pallas import tpu as pltpu
from jax.sharding import PartitionSpec as P

H = 12
DH = 64
NB = 32
LEN = 256
ENC = 128
EPSILON = 1e-06
NEGATIVE = -1e30
F32 = jnp.float32
BF16 = jnp.bfloat16
VMEM_LIMIT = 56 * 1024 * 1024


def product(left, right):
    return jnp.dot(left, right, preferred_element_type=F32)


def product_tn(left, right):
    return lax.dot_general(left, right, (((0,), (0,)), ((), ())), preferred_element_type=F32)


def product_nt(left, right):
    return lax.dot_general(left, right, (((1,), (1,)), ((), ())), preferred_element_type=F32)


def exact_nt(left, right):
    return lax.dot_general(
        left, right, (((1,), (1,)), ((), ())), preferred_element_type=F32, precision=lax.Precision.HIGHEST
    )


def inverse_rms(values):
    return lax.rsqrt(jnp.mean(values * values, axis=-1, keepdims=True) + EPSILON)


def norm_back(values, gain, upstream):
    inverse = inverse_rms(values)
    scaled = upstream * gain
    inner = jnp.mean(scaled * values, axis=-1, keepdims=True)
    grad_values = inverse * scaled - values * (inverse * inverse * inverse * inner)
    grad_gain = jnp.sum(upstream * values * inverse, axis=0, keepdims=True)
    return grad_values, grad_gain


def both_heads(pair):
    first = lax.broadcasted_iota(jnp.int32, pair.shape, 1) < DH
    zero = jnp.zeros_like(pair)
    return jnp.concatenate([jnp.where(first, pair, zero), jnp.where(first, zero, pair)], axis=0)


def join_heads(stacked):
    rows = stacked.shape[0] // 2
    first = lax.broadcasted_iota(jnp.int32, (rows, stacked.shape[1]), 1) < DH
    return jnp.where(first, stacked[:rows], stacked[rows:])


def softmax(scores):
    expo = jnp.exp(scores - jnp.max(scores, axis=-1, keepdims=True))
    return expo * (1.0 / jnp.sum(expo, axis=-1, keepdims=True))


def attend_back(query, keys, values, probs, upstream):
    upper = both_heads(upstream)
    grad_probs = product_nt(upper, values)
    inner = jnp.sum(probs * grad_probs, axis=-1, keepdims=True)
    grad_scores = (probs * (grad_probs - inner)).astype(BF16)
    grad_query = join_heads(product(grad_scores, keys)).astype(BF16)
    grad_keys = product_tn(grad_scores, both_heads(query)).astype(BF16)
    grad_values = product_tn(probs.astype(BF16), upper).astype(BF16)
    return grad_query, grad_keys, grad_values, grad_scores


def bucket_onehot(buckets):
    return (lax.broadcasted_iota(jnp.int32, (NB, LEN), 0) == buckets).astype(F32)


def reversal():
    shape = (LEN, LEN)
    return (
        lax.broadcasted_iota(jnp.int32, shape, 0) + lax.broadcasted_iota(jnp.int32, shape, 1) == LEN - 1
    ).astype(BF16)


class Plan:
    LINE = (0, 8, 4, 12)
    BITS = ((1, 2), (2, 1))

    def __init__(self, mesh, rows):
        self.size = mesh.shape["dp"]
        self.rows = rows
        self.staged = self.size == 16 and rows % 16 == 0
        self.pieces = 4 if self.staged else 1

    def line(self, here, direct):
        if direct:
            return [((here - 4 * step) & 12) | (here & 3) for step in range(4)]
        return [here ^ mask for mask in self.LINE]

    def spans(self, direct):
        if not self.staged:
            return [(0, 0, 0, self.size * self.rows, None)]
        here = lax.axis_index("dp")
        result = []
        for half, (first_bit, second_bit) in enumerate(self.BITS):
            for far in range(2):
                line = self.line(here ^ (far * second_bit), direct)
                for number, device in enumerate(line + [other ^ first_bit for other in line]):
                    first = pl.multiple_of(device * self.rows, 16)
                    result.append((2 * half + far, number * self.rows, first, self.rows, half))
        return result

    def copies(self, pieces, whole, sems, forward, direct):
        width = whole.shape[1] // 2
        result = []
        for number, (piece, row, first, rows, half) in enumerate(self.spans(direct)):
            columns = pl.ds(0, 2 * width) if half is None else pl.ds(half * width, width)
            part = pieces[piece].at[pl.ds(row, rows), :]
            block = whole.at[pl.ds(first, rows), columns]
            ends = (part, block) if forward else (block, part)
            result.append(pltpu.make_async_copy(*ends, sems.at[number]))
        return result

    def n_copies(self):
        return 32 if self.staged else 1

    def piece_shapes(self, width):
        if self.staged:
            return [jax.ShapeDtypeStruct((8 * self.rows, width // 2), BF16)] * 4
        return [jax.ShapeDtypeStruct((self.size * self.rows, width), BF16)]


def swap(block, axis_bit, size):
    return lax.ppermute(block, "dp", [(i, i ^ axis_bit) for i in range(size)])


def shift_z(block, step):
    return lax.ppermute(block, "dp", [(i, ((i + 4 * step) & 12) | (i & 3)) for i in range(16)])


def after(value, *events):
    return lax.optimization_barrier((value, *events))[0] if events else value


def wide(value):
    return value.astype(F32)


def stack(*blocks):
    return jnp.concatenate(blocks, axis=0)


class Gather:
    def __init__(self, plan, block, *events, direct=False):
        self.plan, self.direct = plan, direct
        block = after(block, *events)
        if plan.staged and direct:
            self.block, self.got = block, [shift_z(block, step) for step in (1, 2, 3)]
        elif plan.staged:
            self.block, self.got = block, swap(block, 8, 16)
        else:
            self.got = lax.all_gather(block, "dp", axis=0, tiled=True)

    def line(self, *events):
        if self.plan.staged:
            self.block = stack(self.block, after(self.got, *events))
            self.sent = [self.block]
            self.got = swap(self.block, 4, 16)

    def near(self, *events):
        if self.plan.staged:
            gots = self.got if self.direct else [self.got]
            whole = stack(self.block, *(after(got, *events) for got in gots))
            width = whole.shape[1] // 2
            self.sent = self.halves = [whole[:, :width], whole[:, width:]]
            self.gots = [swap(half, bits[0], 16) for half, bits in zip(self.halves, Plan.BITS)]
            self.got = self.gots[0]

    def far(self, *events):
        if self.plan.staged:
            self.sent = self.halves = [stack(half, after(got, *events)) for half, got in zip(self.halves, self.gots)]
            self.gots = [swap(half, bits[1], 16) for half, bits in zip(self.halves, Plan.BITS)]
            self.got = self.gots[0]

    def ready(self):
        return self.sent if self.plan.staged else []

    def pieces(self):
        if not self.plan.staged:
            return [self.got]
        return [self.halves[0], self.gots[0], self.halves[1], self.gots[1]]


class Scatter:
    def __init__(self, plan, pieces, *events):
        self.plan = plan
        if plan.staged:
            self.sums = [wide(pieces[0]), wide(pieces[2])]
            self.gots = [
                swap(after(piece, *events), bits[1], 16) for piece, bits in zip((pieces[1], pieces[3]), Plan.BITS)
            ]
            self.got = self.gots[0]
        else:
            self.got = lax.psum_scatter(wide(pieces[0]), "dp", scatter_dimension=0, tiled=True)

    def near(self, *events):
        if self.plan.staged:
            rows = 4 * self.plan.rows
            sums = [one + wide(after(got, *events)) for one, got in zip(self.sums, self.gots)]
            self.sent = [one[rows:].astype(BF16) for one in sums]
            self.gots = [swap(one, bits[0], 16) for one, bits in zip(self.sent, Plan.BITS)]
            self.sums = [one[:rows] for one in sums]
            self.got = self.gots[0]

    def line(self, *events):
        if self.plan.staged:
            rows = 2 * self.plan.rows
            whole = jnp.concatenate(
                [one + wide(after(got, *events)) for one, got in zip(self.sums, self.gots)], axis=1
            )
            self.sent = [whole[rows:].astype(BF16)]
            self.got = swap(self.sent[0], 4, 16)
            self.sums = whole[:rows]

    def direct(self, *events):
        if self.plan.staged:
            rows = self.plan.rows
            whole = jnp.concatenate(
                [one + wide(after(got, *events)) for one, got in zip(self.sums, self.gots)], axis=1
            )
            self.sent = [whole[step * rows : (step + 1) * rows].astype(BF16) for step in (1, 2, 3)]
            gots = [shift_z(one, -step) for step, one in zip((1, 2, 3), self.sent)]
            self.sums = whole[:rows] + wide(gots[0]) + wide(gots[1])
            self.got = gots[2]

    def last(self, *events):
        if self.plan.staged:
            rows = self.plan.rows
            whole = self.sums + wide(after(self.got, *events))
            self.sent = [whole[rows:].astype(BF16)]
            self.got = swap(self.sent[0], 8, 16)
            self.sums = whole[:rows]

    def ready(self):
        return self.sent if self.plan.staged else []

    def total(self, *events):
        if self.plan.staged:
            return self.sums + wide(after(self.got, *events))
        return self.got


def other_core(block):
    return lax.ppermute(block, "tensor", [(0, 1), (1, 0)])


def sum_everywhere(plan, block, events):
    if plan.size & (plan.size - 1):
        return lax.psum(block, "dp")
    bits = [1 << place for place in range(plan.size.bit_length() - 1)]
    for bit in [2, 1] + bits[2:] if plan.staged else bits:
        block = block + swap(after(block, *events.get(bit, ())), bit, plan.size)
    return block


VM = pl.BlockSpec(memory_space=pltpu.VMEM)
SM = pl.BlockSpec(memory_space=pltpu.SMEM)
ANY = pl.BlockSpec(memory_space=pl.ANY)


def call(body, name, inputs, specs, outputs, out_specs, scratch, flops):
    nbytes = sum(a.size * a.dtype.itemsize for a in inputs) + sum(
        a.size * jnp.dtype(a.dtype).itemsize for a in outputs
    )
    return pl.pallas_call(
        body,
        name=name,
        out_shape=outputs,
        in_specs=specs,
        out_specs=out_specs,
        scratch_shapes=scratch,
        compiler_params=pltpu.CompilerParams(vmem_limit_bytes=VMEM_LIMIT),
        cost_estimate=pl.CostEstimate(flops=10**10, bytes_accessed=nbytes, transcendentals=0),
    )(*inputs)


def shape(*dims, dtype=F32):
    return jax.ShapeDtypeStruct(dims, dtype)


def rows_of(mine, other, core):
    first = jnp.where(core == 0, mine, other)
    second = jnp.where(core == 0, other, mine)
    return jnp.concatenate([first, second], axis=0)


def wide_sum(mine, other):
    return mine[...].astype(F32) + other[...].astype(F32)


def pack(name, groups):
    arrays = [block[0] for group in groups for block in group]
    rows = arrays[0].shape[0]
    if rows % 16:
        return [jnp.concatenate([m[:, at : at + size] for m, at, size in group], axis=1) for group in groups]

    def body(*refs):
        ins, outs = list(refs[: len(arrays)]), refs[len(arrays) :]
        for group, out in zip(groups, outs):
            column = 0
            for _, at, size in group:
                out[:, column : column + size] = ins.pop(0)[:, at : at + size]
                column += size

    return pl.pallas_call(
        body,
        name=name,
        out_shape=[shape(rows, sum(block[2] for block in group), dtype=BF16) for group in groups],
        in_specs=[VM] * len(arrays),
        out_specs=[VM] * len(groups),
        compiler_params=pltpu.CompilerParams(vmem_limit_bytes=VMEM_LIMIT),
    )(*arrays)


def bring(plan, pieces, whole, sems, direct=False):
    copies = plan.copies(pieces, whole, sems, True, direct)
    for copy in copies:
        copy.start()
    return copies


def finish(copies):
    for copy in copies:
        copy.wait()


def hand_out(plan, pieces, whole, sems, direct=False):
    copies = plan.copies(pieces, whole, sems, False, direct)
    for copy in copies:
        copy.start()
    finish(copies)


def self_forward(plan, pieces, x_mine, x_other, gain, table, buckets, dec_lengths, owner):
    n = plan.pieces
    d = x_mine.shape[1]
    width = pieces[0].shape[1] // (2 if plan.staged else 4)
    pairs = width // (2 * DH)

    def body(*refs):
        weights = refs[:n]
        xm, xo, g, tab, buck, lens, own = refs[n : n + 7]
        part, normed_ref, qkv, probs_ref, mixed_ref, whole, sems = refs[n + 7 :]
        copies = bring(plan, weights, whole, sems, True)
        core = lax.axis_index("tensor")
        length = lens[own[lax.axis_index("dp")]]
        x = rows_of(xm[...], xo[...], core).astype(F32)
        normed = (x * inverse_rms(x) * g[...]).astype(BF16)
        normed_ref[...] = normed
        distances = lax.dot_general(
            tab[...], bucket_onehot(buck[...]), (((1,), (0,)), ((), ())),
            preferred_element_type=F32, precision=lax.Precision.HIGHEST,
        )
        heads = 2 * pairs
        mine = distances[:heads]
        for other in range(1, H // heads):
            mine = jnp.where(core == other, distances[other * heads : (other + 1) * heads], mine)
        row = lax.broadcasted_iota(jnp.int32, (2 * LEN, LEN), 0) & (LEN - 1)
        key = lax.broadcasted_iota(jnp.int32, (2 * LEN, LEN), 1)
        allowed = (key <= row) & (key < length)
        finish(copies)
        qkv[...] = product(normed, whole[:, : 3 * width]).astype(BF16)
        for pair in range(pairs):
            lanes = slice(pair * 128, (pair + 1) * 128)
            query = qkv[:, lanes]
            keys = qkv[:, width + pair * 128 : width + (pair + 1) * 128]
            values = qkv[:, 2 * width + pair * 128 : 2 * width + (pair + 1) * 128]
            extra = jnp.concatenate(
                [
                    pltpu.roll(
                        jnp.broadcast_to(mine[h : h + 1], (LEN, LEN)), 0, 1, stride=1, stride_axis=0
                    )
                    for h in (2 * pair, 2 * pair + 1)
                ],
                axis=0,
            )
            scores = product_nt(both_heads(query), keys) + extra
            probs = softmax(jnp.where(allowed, scores, NEGATIVE))
            probs_ref[pl.ds(pair * 2 * LEN, 2 * LEN), :] = probs
            mixed_ref[:, lanes] = join_heads(product(probs.astype(BF16), values)).astype(BF16)
        part[...] = product_nt(mixed_ref[...], whole[:, 3 * width :]).astype(BF16)

    outputs = [
        shape(LEN, d, dtype=BF16),
        shape(LEN, d, dtype=BF16),
        shape(LEN, 3 * width, dtype=BF16),
        shape(pairs * 2 * LEN, LEN),
        shape(LEN, width, dtype=BF16),
    ]
    return call(
        body,
        "self_forward",
        [*pieces, x_mine, x_other, gain, table, buckets, dec_lengths, owner],
        [ANY] * n + [VM] * 5 + [SM] * 2,
        outputs,
        [VM] * 5,
        [pltpu.VMEM((d, 4 * width), BF16), pltpu.SemaphoreType.DMA((plan.n_copies(),))],
        2 * LEN * d * 4 * width + 8 * LEN * LEN * width,
    )


def cross_forward(plan, pieces, x_mine, x_other, part_mine, part_other, gain, e_mine, e_other, enc_lengths, owner):
    n = plan.pieces
    d = x_mine.shape[1]
    width = pieces[0].shape[1] // (2 if plan.staged else 4)
    pairs = width // (2 * DH)

    def body(*refs):
        weights = refs[:n]
        xm, xo, pm, po, g, em, eo, lens, own = refs[n : n + 9]
        part, after_ref, normed_ref, q_ref, kv, probs_ref, mixed_ref, whole, sems = refs[n + 9 :]
        copies = bring(plan, weights, whole, sems)
        core = lax.axis_index("tensor")
        length = lens[own[lax.axis_index("dp")]]
        after = rows_of(xm[...], xo[...], core).astype(F32) + wide_sum(pm, po)
        after_ref[...] = after
        normed = (after * inverse_rms(after) * g[...]).astype(BF16)
        normed_ref[...] = normed
        allowed = lax.broadcasted_iota(jnp.int32, (2 * LEN, ENC), 1) < length
        finish(copies)
        kv[...] = product(rows_of(em[...], eo[...], core), whole[:, width : 3 * width]).astype(BF16)
        q_ref[...] = product(normed, whole[:, :width]).astype(BF16)
        for pair in range(pairs):
            lanes = slice(pair * 128, (pair + 1) * 128)
            keys = kv[:, lanes]
            values = kv[:, width + pair * 128 : width + (pair + 1) * 128]
            scores = product_nt(both_heads(q_ref[:, lanes]), keys)
            probs = softmax(jnp.where(allowed, scores, NEGATIVE))
            probs_ref[pl.ds(pair * 2 * LEN, 2 * LEN), :] = probs
            mixed_ref[:, lanes] = join_heads(product(probs.astype(BF16), values)).astype(BF16)
        part[...] = product_nt(mixed_ref[...], whole[:, 3 * width :]).astype(BF16)

    outputs = [
        shape(LEN, d, dtype=BF16),
        shape(LEN, d),
        shape(LEN, d, dtype=BF16),
        shape(LEN, width, dtype=BF16),
        shape(ENC, 2 * width, dtype=BF16),
        shape(pairs * 2 * LEN, ENC),
        shape(LEN, width, dtype=BF16),
    ]
    return call(
        body,
        "cross_forward",
        [*pieces, x_mine, x_other, part_mine, part_other, gain, e_mine, e_other, enc_lengths, owner],
        [ANY] * n + [VM] * 7 + [SM] * 2,
        outputs,
        [VM] * 7,
        [pltpu.VMEM((d, 4 * width), BF16), pltpu.SemaphoreType.DMA((plan.n_copies(),))],
        2 * LEN * d * 3 * width + 4 * LEN * ENC * width,
    )


GELU_C = 0.7978845608028654


def feed_units(normed, top, whole, grads, units):
    gate = product(normed, whole[:, :units])
    upper = product(normed, whole[:, units : 2 * units])
    square = gate * gate
    tanh = jnp.tanh(GELU_C * gate * (1.0 + 0.044715 * square))
    half = 0.5 * (1.0 + tanh)
    gelu = gate * half
    slope = half + 0.5 * gate * (1.0 - tanh * tanh) * (GELU_C * (1.0 + 3 * 0.044715 * square))
    hidden = (gelu * upper).astype(BF16)
    grad_hidden = product(top, whole[:, 2 * units :])
    grad_gate = (grad_hidden * upper * slope).astype(BF16)
    grad_up = (grad_hidden * gelu).astype(BF16)
    out = product_nt(hidden, whole[:, 2 * units :])
    back = product_nt(grad_gate, whole[:, :units]) + product_nt(grad_up, whole[:, units : 2 * units])
    grads[:, :units] = product_tn(normed, grad_gate).astype(BF16)
    grads[:, units : 2 * units] = product_tn(normed, grad_up).astype(BF16)
    grads[:, 2 * units :] = product_tn(top, hidden).astype(BF16)
    return out, back


def feed_first(plan, pieces, after_self, part_mine, part_other, gain, c_mine, c_other, dec_lengths, owner):
    n = plan.pieces
    d = after_self.shape[1]
    total = pieces[0].shape[1] * (2 if plan.staged else 1)
    units = total // 3

    def body(*refs):
        weights = refs[:n]
        a_ref, pm, po, g, cm, co, lens, own = refs[n : n + 8]
        after_ref, normed_ref, top_ref, out_ref, back_ref = refs[n + 8 : n + 13]
        grads_out = refs[n + 13 : 2 * n + 13]
        whole, grads, sems = refs[2 * n + 13 :]
        copies = bring(plan, weights, whole, sems)
        core = lax.axis_index("tensor")
        length = lens[own[lax.axis_index("dp")]]
        after = a_ref[...] + wide_sum(pm, po)
        after_ref[...] = after
        normed = (after * inverse_rms(after) * g[...]).astype(BF16)
        normed_ref[...] = normed
        cot = rows_of(cm[...], co[...], core)
        valid = lax.broadcasted_iota(jnp.int32, cot.shape, 0) < length
        top = jnp.where(valid, cot.astype(F32), 0.0).astype(BF16)
        top_ref[...] = top
        finish(copies)
        out_ref[...], back_ref[...] = feed_units(normed, top, whole, grads, units)
        hand_out(plan, grads_out, grads, sems)

    outputs = [
        shape(LEN, d),
        shape(LEN, d, dtype=BF16),
        shape(LEN, d, dtype=BF16),
        shape(LEN, d),
        shape(LEN, d),
        *plan.piece_shapes(total),
    ]
    return call(
        body,
        "feed_first",
        [*pieces, after_self, part_mine, part_other, gain, c_mine, c_other, dec_lengths, owner],
        [ANY] * n + [VM] * 6 + [SM] * 2,
        outputs,
        [VM] * 5 + [ANY] * n,
        [
            pltpu.VMEM((d, total), BF16),
            pltpu.VMEM((d, total), BF16),
            pltpu.SemaphoreType.DMA((plan.n_copies(),)),
        ],
        2 * LEN * d * 9 * units,
    )


def feed_second(plan, pieces, normed, top, out, back):
    n = plan.pieces
    d = normed.shape[1]
    total = pieces[0].shape[1] * (2 if plan.staged else 1)
    units = total // 3

    def body(*refs):
        weights = refs[:n]
        normed_ref, top_ref, out_ref, back_ref = refs[n : n + 4]
        sums = refs[n + 4]
        grads_out = refs[n + 5 : 2 * n + 5]
        whole, grads, sems = refs[2 * n + 5 :]
        copies = bring(plan, weights, whole, sems)
        finish(copies)
        more_out, more_back = feed_units(normed_ref[...], top_ref[...], whole, grads, units)
        sums[:LEN, :] = (back_ref[...] + more_back).astype(BF16)
        sums[LEN:, :] = (out_ref[...] + more_out).astype(BF16)
        hand_out(plan, grads_out, grads, sems)

    return call(
        body,
        "feed_second",
        [*pieces, normed, top, out, back],
        [ANY] * n + [VM] * 4,
        [shape(2 * LEN, d, dtype=BF16), *plan.piece_shapes(total)],
        [VM] + [ANY] * n,
        [
            pltpu.VMEM((d, total), BF16),
            pltpu.VMEM((d, total), BF16),
            pltpu.SemaphoreType.DMA((plan.n_copies(),)),
        ],
        2 * LEN * d * 9 * units,
    )


def cross_backward(
    plan, pieces, after_cross, top, sums_mine, sums_other, gain, normed, query, kv, probs, mixed, e_mine, e_other
):
    n = plan.pieces
    d = normed.shape[1]
    width = query.shape[1]
    pairs = width // (2 * DH)
    half_rows = LEN // 2

    def body(*refs):
        weights = refs[:n]
        after, top_ref, sm, so, g, normed_ref, q_ref, kv_ref, probs_ref, mixed_ref, em, eo = refs[n : n + 12]
        total_ref, sums, layer_out, grad_gain = refs[n + 12 : n + 16]
        grads_out = refs[n + 16 : 2 * n + 16]
        whole, grads, grad_q, grad_kv, sems = refs[2 * n + 16 :]
        copies = bring(plan, weights, whole, sems)
        core = lax.axis_index("tensor")
        back, gain_row = norm_back(after[...], g[...], wide_sum(sm.at[:LEN], so.at[:LEN]))
        grad_gain[...] = gain_row
        total = top_ref[...].astype(F32) + back
        total_ref[...] = total
        upstream = total.astype(BF16)
        first = pl.multiple_of(core * half_rows, half_rows)
        tail = pl.ds(pl.multiple_of(LEN + core * half_rows, half_rows), half_rows)
        layer_out[...] = (
            after[pl.ds(first, half_rows), :] + sm[tail, :].astype(F32) + so[tail, :].astype(F32)
        ).astype(BF16)
        states = rows_of(em[...], eo[...], core)
        finish(copies)
        grad_mixed = product(upstream, whole[:, 3 * width :]).astype(BF16)
        for pair in range(pairs):
            lanes = slice(pair * 128, (pair + 1) * 128)
            lanes_v = slice(width + pair * 128, width + (pair + 1) * 128)
            gq, gk, gv, _ = attend_back(
                q_ref[:, lanes],
                kv_ref[:, lanes],
                kv_ref[:, lanes_v],
                probs_ref[pl.ds(pair * 2 * LEN, 2 * LEN), :],
                grad_mixed[:, lanes],
            )
            grad_q[:, lanes] = gq
            grad_kv[:, lanes] = gk
            grad_kv[:, lanes_v] = gv
        sums[:LEN, :] = product_nt(grad_q[...], whole[:, :width]).astype(BF16)
        sums[LEN:, :] = product_nt(grad_kv[...], whole[:, width : 3 * width]).astype(BF16)
        grads[:, :width] = product_tn(normed_ref[...], grad_q[...]).astype(BF16)
        grads[:, width : 3 * width] = product_tn(states, grad_kv[...]).astype(BF16)
        grads[:, 3 * width :] = product_tn(upstream, mixed_ref[...]).astype(BF16)
        hand_out(plan, grads_out, grads, sems)

    return call(
        body,
        "cross_backward",
        [*pieces, after_cross, top, sums_mine, sums_other, gain, normed, query, kv, probs, mixed, e_mine, e_other],
        [ANY] * n + [VM] * 12,
        [
            shape(LEN, d),
            shape(LEN + ENC, d, dtype=BF16),
            shape(half_rows, d, dtype=BF16),
            shape(1, d),
            *plan.piece_shapes(4 * width),
        ],
        [VM] * 4 + [ANY] * n,
        [
            pltpu.VMEM((d, 4 * width), BF16),
            pltpu.VMEM((d, 4 * width), BF16),
            pltpu.VMEM((LEN, width), BF16),
            pltpu.VMEM((ENC, 2 * width), BF16),
            pltpu.SemaphoreType.DMA((plan.n_copies(),)),
        ],
        2 * LEN * d * 6 * width + 10 * LEN * ENC * width,
    )


def table_rows(per_distance, buckets, core, d):
    heads = len(per_distance)
    rows = jnp.concatenate(per_distance + [jnp.zeros_like(per_distance[0])] * (8 - heads), axis=0)
    lane = lax.broadcasted_iota(jnp.int32, (d, LEN), 0)
    table = exact_nt(rows, ((lane & (NB - 1)) == buckets).astype(F32))
    lane = lax.broadcasted_iota(jnp.int32, (8, d), 1)
    head = lax.broadcasted_iota(jnp.int32, (8, d), 0)
    kept = ((lane >> 5) == head + core * heads) & (head < heads)
    row = jnp.sum(jnp.where(kept, table, 0.0), axis=0, keepdims=True)
    high = row.astype(BF16)
    low = (row - high.astype(F32)).astype(BF16)
    return jnp.concatenate([high, low, jnp.zeros((14, d), BF16)], axis=0)


def self_backward(
    plan, pieces, total_cross, after_self, sums_mine, sums_other, gain, normed, qkv, probs, mixed, buckets
):
    n = plan.pieces
    d = normed.shape[1]
    width = mixed.shape[1]
    pairs = width // (2 * DH)
    half_enc = ENC // 2

    def body(*refs):
        weights = refs[:n]
        tc, after, sm, so, g, normed_ref, qkv_ref, probs_ref, mixed_ref, buck = refs[n : n + 10]
        total_ref, sums, states_out, grad_gain = refs[n + 10 : n + 14]
        grads_out = refs[n + 14 : 2 * n + 14]
        whole, grads, grad_qkv, sems = refs[2 * n + 14 :]
        copies = bring(plan, weights, whole, sems, True)
        core = lax.axis_index("tensor")
        back, gain_row = norm_back(after[...], g[...], wide_sum(sm.at[:LEN], so.at[:LEN]))
        grad_gain[...] = gain_row
        total = tc[...] + back
        total_ref[...] = total
        upstream = total.astype(BF16)
        tail = pl.ds(pl.multiple_of(LEN + core * half_enc, half_enc), half_enc)
        states_out[...] = sm[tail, :].astype(F32) + so[tail, :].astype(F32)
        finish(copies)
        grad_mixed = product(upstream, whole[:, 3 * width :]).astype(BF16)
        backwards = reversal()
        per_distance = []
        for pair in range(pairs):
            lanes = slice(pair * 128, (pair + 1) * 128)
            lanes_k = slice(width + pair * 128, width + (pair + 1) * 128)
            lanes_v = slice(2 * width + pair * 128, 2 * width + (pair + 1) * 128)
            gq, gk, gv, gs = attend_back(
                qkv_ref[:, lanes],
                qkv_ref[:, lanes_k],
                qkv_ref[:, lanes_v],
                probs_ref[pl.ds(pair * 2 * LEN, 2 * LEN), :],
                grad_mixed[:, lanes],
            )
            grad_qkv[:, lanes] = gq
            grad_qkv[:, lanes_k] = gk
            grad_qkv[:, lanes_v] = gv
            turned_scores = product(gs, backwards)
            for h in range(2):
                rolled = pltpu.roll(
                    turned_scores[h * LEN : (h + 1) * LEN], 0, 1, stride=1, stride_axis=0
                )
                per_distance.append(jnp.sum(rolled, axis=0, keepdims=True))
        sums[:LEN, :] = product_nt(grad_qkv[...], whole[:, : 3 * width]).astype(BF16)
        sums[LEN:, :] = table_rows(per_distance, buck[...], core, d)
        grads[:, : 3 * width] = product_tn(normed_ref[...], grad_qkv[...]).astype(BF16)
        grads[:, 3 * width :] = product_tn(upstream, mixed_ref[...]).astype(BF16)
        hand_out(plan, grads_out, grads, sems, True)

    return call(
        body,
        "self_backward",
        [*pieces, total_cross, after_self, sums_mine, sums_other, gain, normed, qkv, probs, mixed, buckets],
        [ANY] * n + [VM] * 10,
        [
            shape(LEN, d),
            shape(LEN + 16, d, dtype=BF16),
            shape(half_enc, d),
            shape(1, d),
            *plan.piece_shapes(4 * width),
        ],
        [VM] * 4 + [ANY] * n,
        [
            pltpu.VMEM((d, 4 * width), BF16),
            pltpu.VMEM((d, 4 * width), BF16),
            pltpu.VMEM((LEN, 3 * width), BF16),
            pltpu.SemaphoreType.DMA((plan.n_copies(),)),
        ],
        2 * LEN * d * 8 * width + 14 * LEN * LEN * width,
    )


def last_norm(total_self, x_mine, x_other, sums_mine, sums_other, gain, gain_cross_row, gain_feed_row):
    d = total_self.shape[1]
    half_rows = LEN // 2

    def body(total, xm, xo, sm, so, g, ggc, ggf, grad_in, small):
        core = lax.axis_index("tensor")
        x = rows_of(xm[...], xo[...], core).astype(F32)
        back, gain_row = norm_back(x, g[...], wide_sum(sm.at[:LEN], so.at[:LEN]))
        whole = total[...] + back
        grad_in[...] = jnp.where(core == 0, whole[:half_rows], whole[half_rows:])
        table = jnp.sum(wide_sum(sm.at[LEN:], so.at[LEN:]), axis=0, keepdims=True)
        small[...] = jnp.concatenate([gain_row, ggc[...], ggf[...], table, jnp.zeros((4, d), F32)], axis=0)

    return call(
        body,
        "last_norm",
        [total_self, x_mine, x_other, sums_mine, sums_other, gain, gain_cross_row, gain_feed_row],
        [VM] * 8,
        [shape(half_rows, d), shape(8, d)],
        [VM] * 2,
        [],
        1 << 24,
    )


def shards(
    mesh,
    layer_in,
    enc_states,
    cotangent,
    gain_self,
    gain_cross,
    gain_feed,
    bias_table,
    self_query,
    self_key,
    self_value,
    self_out,
    cross_query,
    cross_key,
    cross_value,
    cross_out,
    gate_proj,
    up_proj,
    down_proj,
    dec_lengths,
    enc_lengths,
    seq_owner,
    bucket_table,
):
    plan = Plan(mesh, self_query.shape[0])
    d = layer_in.shape[1]
    width = self_query.shape[1]
    units = gate_proj.shape[1] // 2
    g_self, g_cross, g_feed = (g.reshape(1, d) for g in (gain_self, gain_cross, gain_feed))

    def attention_group(query, key, value, out):
        return [(m, 0, width) for m in (query, key, value, out.T)]

    def feed_group(number):
        return [(m, number * units, units) for m in (gate_proj, up_proj, down_proj.T)]

    (block_s,) = pack("pack_self", [attention_group(self_query, self_key, self_value, self_out)])
    block_c, block_f1, block_f2 = pack(
        "pack_rest",
        [attention_group(cross_query, cross_key, cross_value, cross_out), feed_group(0), feed_group(1)],
    )
    x_other = other_core(layer_in)
    e_other = other_core(enc_states)
    c_other = other_core(cotangent)
    buckets = jnp.concatenate([bucket_table[:1], bucket_table[:0:-1]]).reshape(1, LEN)
    buckets_up = jnp.concatenate([bucket_table[1:], bucket_table[:1]]).reshape(1, LEN)

    at_s = Gather(plan, block_s, direct=True)
    at_c = Gather(plan, block_c, x_other, e_other, c_other)
    at_s.near(block_c)
    at_c.line(*at_s.ready())
    at_s.far()
    at_f1 = Gather(plan, block_f1, *at_s.ready())
    at_c.near(*at_s.ready())
    at_f1.line(*at_c.ready())
    at_c.far()
    at_f2 = Gather(plan, block_f2, *at_c.ready())
    at_f1.near(*at_c.ready())
    part_s, normed_s, qkv, probs_s, mixed_s = self_forward(
        plan, at_s.pieces(), layer_in, after(x_other, *at_f1.ready()), g_self, bias_table.T, buckets, dec_lengths,
        seq_owner,
    )
    part_other = other_core(part_s)
    at_f2.line(part_s)
    at_f1.far(part_s)
    part_c, after_self, normed_c, cq, ckv, probs_c, mixed_c = cross_forward(
        plan, at_c.pieces(), layer_in, x_other, part_s, after(part_other, *at_f1.ready()), g_cross, enc_states,
        e_other, enc_lengths, seq_owner,
    )
    part_other = other_core(part_c)
    at_f2.near(part_c)
    at_f2.far()
    after_cross, normed_f, top, out, back, *grads_f1 = feed_first(
        plan, at_f1.pieces(), after_self, part_c, after(part_other, *at_f2.ready()), g_feed, cotangent, c_other,
        dec_lengths, seq_owner,
    )
    sum_f1 = Scatter(plan, grads_f1)
    sums_f, *grads_f2 = feed_second(plan, at_f2.pieces(), normed_f, top, out, back)
    sum_f1.near(sums_f)
    sum_f2 = Scatter(plan, grads_f2)
    total_cross, sums_c, layer_out, gain_feed_row, *grads_c = cross_backward(
        plan, at_c.pieces(), after_cross, top, sums_f, after(other_core(sums_f), *sum_f1.ready()), g_feed, normed_c,
        cq, ckv, probs_c, mixed_c, enc_states, e_other,
    )
    sum_f1.line(sums_c)
    sum_f2.near(sums_c)
    sum_c = Scatter(plan, grads_c)
    total_self, sums_s, grad_states, gain_cross_row, *grads_s = self_backward(
        plan, at_s.pieces(), total_cross, after_self, sums_c, after(other_core(sums_c), *sum_f2.ready()), g_cross,
        normed_s, qkv, probs_s, mixed_s, buckets_up,
    )
    sum_s = Scatter(plan, grads_s)
    sum_c.near(sums_s)
    sums_other = other_core(sums_s)
    sum_f1.last(sums_other, *sum_c.ready())
    grad_in, small = last_norm(
        total_self, layer_in, x_other, sums_s, after(sums_other, *sum_c.ready()), g_self, gain_cross_row,
        gain_feed_row,
    )
    sum_f2.line(small)
    sum_s.near(small)
    near_s = sum_s.ready()
    grad_f1 = sum_f1.total(*near_s)
    sum_f2.last(*near_s)
    sum_c.line(*near_s)
    sum_s.direct()
    line_s = sum_s.ready()
    grad_f2 = sum_f2.total(*line_s)
    sum_c.last(*line_s)
    grad_c = sum_c.total()
    grad_s = sum_s.total()
    small = sum_everywhere(plan, small, {1: near_s, 4: line_s, 8: line_s})
    table_grad = small[3, : H * NB].reshape(H, NB).T

    def columns(block, number, size):
        return block[:, number * size : (number + 1) * size]

    def feed(number):
        return jnp.concatenate([columns(g, number, units) for g in (grad_f1, grad_f2)], axis=1)

    return (
        layer_out,
        grad_in,
        grad_states,
        small[0],
        small[1],
        small[2],
        table_grad,
        columns(grad_s, 0, width),
        columns(grad_s, 1, width),
        columns(grad_s, 2, width),
        columns(grad_s, 3, width).T,
        columns(grad_c, 0, width),
        columns(grad_c, 1, width),
        columns(grad_c, 2, width),
        columns(grad_c, 3, width).T,
        feed(0),
        feed(1),
        feed(2).T,
    )


def solution(mesh):
    rows = P(("dp", "tensor"), None)
    into, out = P("dp", "tensor"), P("tensor", "dp")
    weights = (into, into, into, out, into, into, into, out, into, into, out)
    in_specs = (rows, rows, rows, P(), P(), P(), P(), *weights, P(), P(), P(), P())
    out_specs = (rows, rows, rows, P(), P(), P(), P(), *weights)
    return jax.shard_map(
        functools.partial(shards, mesh), mesh=mesh, in_specs=in_specs, out_specs=out_specs, check_vma=False
    )
```

```python
import functools

import jax
import jax.numpy as jnp
from jax import lax
from jax.experimental import pallas as pl
from jax.experimental.pallas import tpu as pltpu
from jax.sharding import PartitionSpec as P

H = 12
DH = 64
NB = 32
LEN = 256
ENC = 128
EPSILON = 1e-06
NEGATIVE = -1e30
F32 = jnp.float32
BF16 = jnp.bfloat16
VMEM_LIMIT = 56 * 1024 * 1024


def product(left, right):
    return jnp.dot(left, right, preferred_element_type=F32)


def product_tn(left, right):
    return lax.dot_general(left, right, (((0,), (0,)), ((), ())), preferred_element_type=F32)


def product_nt(left, right):
    return lax.dot_general(left, right, (((1,), (1,)), ((), ())), preferred_element_type=F32)


def exact_nt(left, right):
    return lax.dot_general(
        left, right, (((1,), (1,)), ((), ())), preferred_element_type=F32, precision=lax.Precision.HIGHEST
    )


def inverse_rms(values):
    return lax.rsqrt(jnp.mean(values * values, axis=-1, keepdims=True) + EPSILON)


def norm_back(values, gain, upstream):
    inverse = inverse_rms(values)
    scaled = upstream * gain
    inner = jnp.mean(scaled * values, axis=-1, keepdims=True)
    grad_values = inverse * scaled - values * (inverse * inverse * inverse * inner)
    grad_gain = jnp.sum(upstream * values * inverse, axis=0, keepdims=True)
    return grad_values, grad_gain


def both_heads(pair):
    first = lax.broadcasted_iota(jnp.int32, pair.shape, 1) < DH
    zero = jnp.zeros_like(pair)
    return jnp.concatenate([jnp.where(first, pair, zero), jnp.where(first, zero, pair)], axis=0)


def join_heads(stacked):
    rows = stacked.shape[0] // 2
    first = lax.broadcasted_iota(jnp.int32, (rows, stacked.shape[1]), 1) < DH
    return jnp.where(first, stacked[:rows], stacked[rows:])


def softmax(scores):
    expo = jnp.exp(scores - jnp.max(scores, axis=-1, keepdims=True))
    return expo * (1.0 / jnp.sum(expo, axis=-1, keepdims=True))


def attend_back(query, keys, values, probs, upstream):
    upper = both_heads(upstream)
    grad_probs = product_nt(upper, values)
    inner = jnp.sum(probs * grad_probs, axis=-1, keepdims=True)
    grad_scores = (probs * (grad_probs - inner)).astype(BF16)
    grad_query = join_heads(product(grad_scores, keys)).astype(BF16)
    grad_keys = product_tn(grad_scores, both_heads(query)).astype(BF16)
    grad_values = product_tn(probs.astype(BF16), upper).astype(BF16)
    return grad_query, grad_keys, grad_values, grad_scores


def bucket_onehot(buckets):
    return (lax.broadcasted_iota(jnp.int32, (NB, LEN), 0) == buckets).astype(F32)


def reversal():
    shape = (LEN, LEN)
    return (
        lax.broadcasted_iota(jnp.int32, shape, 0) + lax.broadcasted_iota(jnp.int32, shape, 1) == LEN - 1
    ).astype(BF16)


class Plan:
    LINE = (0, 8, 4, 12)
    BITS = ((1, 2), (2, 1))

    def __init__(self, mesh, rows):
        self.size = mesh.shape["dp"]
        self.rows = rows
        self.staged = self.size == 16 and rows % 16 == 0
        self.pieces = 4 if self.staged else 1

    def line(self, here, direct):
        if direct:
            return [((here - 4 * step) & 12) | (here & 3) for step in range(4)]
        return [here ^ mask for mask in self.LINE]

    def spans(self, direct):
        if not self.staged:
            return [(0, 0, 0, self.size * self.rows, None)]
        here = lax.axis_index("dp")
        result = []
        for half, (first_bit, second_bit) in enumerate(self.BITS):
            for far in range(2):
                line = self.line(here ^ (far * second_bit), direct)
                for number, device in enumerate(line + [other ^ first_bit for other in line]):
                    first = pl.multiple_of(device * self.rows, 16)
                    result.append((2 * half + far, number * self.rows, first, self.rows, half))
        return result

    def copies(self, pieces, whole, sems, forward, direct):
        width = whole.shape[1] // 2
        result = []
        for number, (piece, row, first, rows, half) in enumerate(self.spans(direct)):
            columns = pl.ds(0, 2 * width) if half is None else pl.ds(half * width, width)
            part = pieces[piece].at[pl.ds(row, rows), :]
            block = whole.at[pl.ds(first, rows), columns]
            ends = (part, block) if forward else (block, part)
            result.append(pltpu.make_async_copy(*ends, sems.at[number]))
        return result

    def n_copies(self):
        return 32 if self.staged else 1

    def piece_shapes(self, width):
        if self.staged:
            return [jax.ShapeDtypeStruct((8 * self.rows, width // 2), BF16)] * 4
        return [jax.ShapeDtypeStruct((self.size * self.rows, width), BF16)]


def swap(block, axis_bit, size):
    return lax.ppermute(block, "dp", [(i, i ^ axis_bit) for i in range(size)])


def shift_z(block, step):
    return lax.ppermute(block, "dp", [(i, ((i + 4 * step) & 12) | (i & 3)) for i in range(16)])


def after(value, *events):
    return lax.optimization_barrier((value, *events))[0] if events else value


def wide(value):
    return value.astype(F32)


def stack(*blocks):
    return jnp.concatenate(blocks, axis=0)


class Gather:
    def __init__(self, plan, block, *events, direct=False):
        self.plan, self.direct = plan, direct
        block = after(block, *events)
        if plan.staged and direct:
            self.block, self.got = block, [shift_z(block, step) for step in (1, 2, 3)]
        elif plan.staged:
            self.block, self.got = block, swap(block, 8, 16)
        else:
            self.got = lax.all_gather(block, "dp", axis=0, tiled=True)

    def line(self, *events):
        if self.plan.staged:
            self.block = stack(self.block, after(self.got, *events))
            self.sent = [self.block]
            self.got = swap(self.block, 4, 16)

    def near(self, *events):
        if self.plan.staged:
            gots = self.got if self.direct else [self.got]
            whole = stack(self.block, *(after(got, *events) for got in gots))
            width = whole.shape[1] // 2
            self.sent = self.halves = [whole[:, :width], whole[:, width:]]
            self.gots = [swap(half, bits[0], 16) for half, bits in zip(self.halves, Plan.BITS)]
            self.got = self.gots[0]

    def far(self, *events):
        if self.plan.staged:
            self.sent = self.halves = [stack(half, after(got, *events)) for half, got in zip(self.halves, self.gots)]
            self.gots = [swap(half, bits[1], 16) for half, bits in zip(self.halves, Plan.BITS)]
            self.got = self.gots[0]

    def ready(self):
        return self.sent if self.plan.staged else []

    def pieces(self):
        if not self.plan.staged:
            return [self.got]
        return [self.halves[0], self.gots[0], self.halves[1], self.gots[1]]


class Scatter:
    def __init__(self, plan, pieces, *events):
        self.plan = plan
        if plan.staged:
            self.sums = [wide(pieces[0]), wide(pieces[2])]
            self.gots = [
                swap(after(piece, *events), bits[1], 16) for piece, bits in zip((pieces[1], pieces[3]), Plan.BITS)
            ]
            self.got = self.gots[0]
        else:
            self.got = lax.psum_scatter(wide(pieces[0]), "dp", scatter_dimension=0, tiled=True)

    def near(self, *events):
        if self.plan.staged:
            rows = 4 * self.plan.rows
            sums = [one + wide(after(got, *events)) for one, got in zip(self.sums, self.gots)]
            self.sent = [one[rows:].astype(BF16) for one in sums]
            self.gots = [swap(one, bits[0], 16) for one, bits in zip(self.sent, Plan.BITS)]
            self.sums = [one[:rows] for one in sums]
            self.got = self.gots[0]

    def line(self, *events):
        if self.plan.staged:
            rows = 2 * self.plan.rows
            whole = jnp.concatenate(
                [one + wide(after(got, *events)) for one, got in zip(self.sums, self.gots)], axis=1
            )
            self.sent = [whole[rows:].astype(BF16)]
            self.got = swap(self.sent[0], 4, 16)
            self.sums = whole[:rows]

    def direct(self, *events):
        if self.plan.staged:
            rows = self.plan.rows
            whole = jnp.concatenate(
                [one + wide(after(got, *events)) for one, got in zip(self.sums, self.gots)], axis=1
            )
            self.sent = [whole[step * rows : (step + 1) * rows].astype(BF16) for step in (1, 2, 3)]
            gots = [shift_z(one, -step) for step, one in zip((1, 2, 3), self.sent)]
            self.sums = whole[:rows] + wide(gots[0]) + wide(gots[1])
            self.got = gots[2]

    def last(self, *events):
        if self.plan.staged:
            rows = self.plan.rows
            whole = self.sums + wide(after(self.got, *events))
            self.sent = [whole[rows:].astype(BF16)]
            self.got = swap(self.sent[0], 8, 16)
            self.sums = whole[:rows]

    def ready(self):
        return self.sent if self.plan.staged else []

    def total(self, *events):
        if self.plan.staged:
            return self.sums + wide(after(self.got, *events))
        return self.got


def other_core(block):
    return lax.ppermute(block, "tensor", [(0, 1), (1, 0)])


def sum_everywhere(plan, block, events):
    if not plan.staged:
        return lax.psum(block, "dp")
    terms = lax.all_to_all(jnp.tile(block, (plan.size, 1)), "dp", 0, 0, tiled=True)
    terms = after(terms, *events)
    return jnp.sum(terms.reshape(plan.size, *block.shape), axis=0)


VM = pl.BlockSpec(memory_space=pltpu.VMEM)
SM = pl.BlockSpec(memory_space=pltpu.SMEM)
ANY = pl.BlockSpec(memory_space=pl.ANY)


def call(body, name, inputs, specs, outputs, out_specs, scratch, flops):
    nbytes = sum(a.size * a.dtype.itemsize for a in inputs) + sum(
        a.size * jnp.dtype(a.dtype).itemsize for a in outputs
    )
    return pl.pallas_call(
        body,
        name=name,
        out_shape=outputs,
        in_specs=specs,
        out_specs=out_specs,
        scratch_shapes=scratch,
        compiler_params=pltpu.CompilerParams(vmem_limit_bytes=VMEM_LIMIT),
        cost_estimate=pl.CostEstimate(flops=0, bytes_accessed=0, transcendentals=0),
    )(*inputs)


def shape(*dims, dtype=F32):
    return jax.ShapeDtypeStruct(dims, dtype)


def rows_of(mine, other, core):
    first = jnp.where(core == 0, mine, other)
    second = jnp.where(core == 0, other, mine)
    return jnp.concatenate([first, second], axis=0)


def wide_sum(mine, other):
    return mine[...].astype(F32) + other[...].astype(F32)


def pack(name, groups):
    arrays = [block[0] for group in groups for block in group]
    rows = arrays[0].shape[0]
    if rows % 16:
        return [jnp.concatenate([m[:, at : at + size] for m, at, size in group], axis=1) for group in groups]

    def body(*refs):
        ins, outs = list(refs[: len(arrays)]), refs[len(arrays) :]
        for group, out in zip(groups, outs):
            column = 0
            for _, at, size in group:
                out[:, column : column + size] = ins.pop(0)[:, at : at + size]
                column += size

    return pl.pallas_call(
        body,
        name=name,
        out_shape=[shape(rows, sum(block[2] for block in group), dtype=BF16) for group in groups],
        in_specs=[VM] * len(arrays),
        out_specs=[VM] * len(groups),
        compiler_params=pltpu.CompilerParams(vmem_limit_bytes=VMEM_LIMIT),
    )(*arrays)


def bring(plan, pieces, whole, sems, direct=False):
    copies = plan.copies(pieces, whole, sems, True, direct)
    for copy in copies:
        copy.start()
    return copies


def finish(copies):
    for copy in copies:
        copy.wait()


def hand_out(plan, pieces, whole, sems, direct=False):
    copies = plan.copies(pieces, whole, sems, False, direct)
    for copy in copies:
        copy.start()
    finish(copies)


def self_forward(plan, pieces, x_mine, x_other, gain, table, buckets, dec_lengths, owner):
    n = plan.pieces
    d = x_mine.shape[1]
    width = pieces[0].shape[1] // (2 if plan.staged else 4)
    pairs = width // (2 * DH)

    def body(*refs):
        weights = refs[:n]
        xm, xo, g, tab, buck, lens, own = refs[n : n + 7]
        part, normed_ref, qkv, probs_ref, mixed_ref, whole, sems = refs[n + 7 :]
        copies = bring(plan, weights, whole, sems, True)
        core = lax.axis_index("tensor")
        length = lens[own[lax.axis_index("dp")]]
        x = rows_of(xm[...], xo[...], core).astype(F32)
        normed = (x * inverse_rms(x) * g[...]).astype(BF16)
        normed_ref[...] = normed
        distances = lax.dot_general(
            tab[...], bucket_onehot(buck[...]), (((1,), (0,)), ((), ())),
            preferred_element_type=F32, precision=lax.Precision.HIGHEST,
        )
        heads = 2 * pairs
        mine = distances[:heads]
        for other in range(1, H // heads):
            mine = jnp.where(core == other, distances[other * heads : (other + 1) * heads], mine)
        row = lax.broadcasted_iota(jnp.int32, (2 * LEN, LEN), 0) & (LEN - 1)
        key = lax.broadcasted_iota(jnp.int32, (2 * LEN, LEN), 1)
        allowed = (key <= row) & (key < length)
        finish(copies)
        qkv[...] = product(normed, whole[:, : 3 * width]).astype(BF16)
        for pair in range(pairs):
            lanes = slice(pair * 128, (pair + 1) * 128)
            query = qkv[:, lanes]
            keys = qkv[:, width + pair * 128 : width + (pair + 1) * 128]
            values = qkv[:, 2 * width + pair * 128 : 2 * width + (pair + 1) * 128]
            extra = jnp.concatenate(
                [
                    pltpu.roll(
                        jnp.broadcast_to(mine[h : h + 1], (LEN, LEN)), 0, 1, stride=1, stride_axis=0
                    )
                    for h in (2 * pair, 2 * pair + 1)
                ],
                axis=0,
            )
            scores = product_nt(both_heads(query), keys) + extra
            probs = softmax(jnp.where(allowed, scores, NEGATIVE))
            probs_ref[pl.ds(pair * 2 * LEN, 2 * LEN), :] = probs
            mixed_ref[:, lanes] = join_heads(product(probs.astype(BF16), values)).astype(BF16)
        part[...] = product_nt(mixed_ref[...], whole[:, 3 * width :]).astype(BF16)

    outputs = [
        shape(LEN, d, dtype=BF16),
        shape(LEN, d, dtype=BF16),
        shape(LEN, 3 * width, dtype=BF16),
        shape(pairs * 2 * LEN, LEN),
        shape(LEN, width, dtype=BF16),
    ]
    return call(
        body,
        "self_forward",
        [*pieces, x_mine, x_other, gain, table, buckets, dec_lengths, owner],
        [ANY] * n + [VM] * 5 + [SM] * 2,
        outputs,
        [VM] * 5,
        [pltpu.VMEM((d, 4 * width), BF16), pltpu.SemaphoreType.DMA((plan.n_copies(),))],
        2 * LEN * d * 4 * width + 8 * LEN * LEN * width,
    )


def cross_forward(plan, pieces, x_mine, x_other, part_mine, part_other, gain, e_mine, e_other, enc_lengths, owner):
    n = plan.pieces
    d = x_mine.shape[1]
    width = pieces[0].shape[1] // (2 if plan.staged else 4)
    pairs = width // (2 * DH)

    def body(*refs):
        weights = refs[:n]
        xm, xo, pm, po, g, em, eo, lens, own = refs[n : n + 9]
        part, after_ref, normed_ref, q_ref, kv, probs_ref, mixed_ref, whole, sems = refs[n + 9 :]
        copies = bring(plan, weights, whole, sems)
        core = lax.axis_index("tensor")
        length = lens[own[lax.axis_index("dp")]]
        after = rows_of(xm[...], xo[...], core).astype(F32) + wide_sum(pm, po)
        after_ref[...] = after
        normed = (after * inverse_rms(after) * g[...]).astype(BF16)
        normed_ref[...] = normed
        allowed = lax.broadcasted_iota(jnp.int32, (2 * LEN, ENC), 1) < length
        finish(copies)
        kv[...] = product(rows_of(em[...], eo[...], core), whole[:, width : 3 * width]).astype(BF16)
        q_ref[...] = product(normed, whole[:, :width]).astype(BF16)
        for pair in range(pairs):
            lanes = slice(pair * 128, (pair + 1) * 128)
            keys = kv[:, lanes]
            values = kv[:, width + pair * 128 : width + (pair + 1) * 128]
            scores = product_nt(both_heads(q_ref[:, lanes]), keys)
            probs = softmax(jnp.where(allowed, scores, NEGATIVE))
            probs_ref[pl.ds(pair * 2 * LEN, 2 * LEN), :] = probs
            mixed_ref[:, lanes] = join_heads(product(probs.astype(BF16), values)).astype(BF16)
        part[...] = product_nt(mixed_ref[...], whole[:, 3 * width :]).astype(BF16)

    outputs = [
        shape(LEN, d, dtype=BF16),
        shape(LEN, d),
        shape(LEN, d, dtype=BF16),
        shape(LEN, width, dtype=BF16),
        shape(ENC, 2 * width, dtype=BF16),
        shape(pairs * 2 * LEN, ENC),
        shape(LEN, width, dtype=BF16),
    ]
    return call(
        body,
        "cross_forward",
        [*pieces, x_mine, x_other, part_mine, part_other, gain, e_mine, e_other, enc_lengths, owner],
        [ANY] * n + [VM] * 7 + [SM] * 2,
        outputs,
        [VM] * 7,
        [pltpu.VMEM((d, 4 * width), BF16), pltpu.SemaphoreType.DMA((plan.n_copies(),))],
        2 * LEN * d * 3 * width + 4 * LEN * ENC * width,
    )


GELU_C = 0.7978845608028654


def feed_units(normed, top, whole, grads, units):
    gate = product(normed, whole[:, :units])
    upper = product(normed, whole[:, units : 2 * units])
    square = gate * gate
    tanh = jnp.tanh(GELU_C * gate * (1.0 + 0.044715 * square))
    half = 0.5 * (1.0 + tanh)
    gelu = gate * half
    slope = half + 0.5 * gate * (1.0 - tanh * tanh) * (GELU_C * (1.0 + 3 * 0.044715 * square))
    hidden = (gelu * upper).astype(BF16)
    grad_hidden = product(top, whole[:, 2 * units :])
    grad_gate = (grad_hidden * upper * slope).astype(BF16)
    grad_up = (grad_hidden * gelu).astype(BF16)
    out = product_nt(hidden, whole[:, 2 * units :])
    back = product_nt(grad_gate, whole[:, :units]) + product_nt(grad_up, whole[:, units : 2 * units])
    grads[:, :units] = product_tn(normed, grad_gate).astype(BF16)
    grads[:, units : 2 * units] = product_tn(normed, grad_up).astype(BF16)
    grads[:, 2 * units :] = product_tn(top, hidden).astype(BF16)
    return out, back


def feed_first(plan, pieces, after_self, part_mine, part_other, gain, c_mine, c_other, dec_lengths, owner):
    n = plan.pieces
    d = after_self.shape[1]
    total = pieces[0].shape[1] * (2 if plan.staged else 1)
    units = total // 3

    def body(*refs):
        weights = refs[:n]
        a_ref, pm, po, g, cm, co, lens, own = refs[n : n + 8]
        after_ref, normed_ref, top_ref, out_ref, back_ref = refs[n + 8 : n + 13]
        grads_out = refs[n + 13 : 2 * n + 13]
        whole, grads, sems = refs[2 * n + 13 :]
        copies = bring(plan, weights, whole, sems)
        core = lax.axis_index("tensor")
        length = lens[own[lax.axis_index("dp")]]
        after = a_ref[...] + wide_sum(pm, po)
        after_ref[...] = after
        normed = (after * inverse_rms(after) * g[...]).astype(BF16)
        normed_ref[...] = normed
        cot = rows_of(cm[...], co[...], core)
        valid = lax.broadcasted_iota(jnp.int32, cot.shape, 0) < length
        top = jnp.where(valid, cot.astype(F32), 0.0).astype(BF16)
        top_ref[...] = top
        finish(copies)
        out_ref[...], back_ref[...] = feed_units(normed, top, whole, grads, units)
        hand_out(plan, grads_out, grads, sems)

    outputs = [
        shape(LEN, d),
        shape(LEN, d, dtype=BF16),
        shape(LEN, d, dtype=BF16),
        shape(LEN, d),
        shape(LEN, d),
        *plan.piece_shapes(total),
    ]
    return call(
        body,
        "feed_first",
        [*pieces, after_self, part_mine, part_other, gain, c_mine, c_other, dec_lengths, owner],
        [ANY] * n + [VM] * 6 + [SM] * 2,
        outputs,
        [VM] * 5 + [ANY] * n,
        [
            pltpu.VMEM((d, total), BF16),
            pltpu.VMEM((d, total), BF16),
            pltpu.SemaphoreType.DMA((plan.n_copies(),)),
        ],
        2 * LEN * d * 9 * units,
    )


def feed_second(plan, pieces, normed, top, out, back):
    n = plan.pieces
    d = normed.shape[1]
    total = pieces[0].shape[1] * (2 if plan.staged else 1)
    units = total // 3

    def body(*refs):
        weights = refs[:n]
        normed_ref, top_ref, out_ref, back_ref = refs[n : n + 4]
        sums = refs[n + 4]
        grads_out = refs[n + 5 : 2 * n + 5]
        whole, grads, sems = refs[2 * n + 5 :]
        copies = bring(plan, weights, whole, sems)
        finish(copies)
        more_out, more_back = feed_units(normed_ref[...], top_ref[...], whole, grads, units)
        sums[:LEN, :] = (back_ref[...] + more_back).astype(BF16)
        sums[LEN:, :] = (out_ref[...] + more_out).astype(BF16)
        hand_out(plan, grads_out, grads, sems)

    return call(
        body,
        "feed_second",
        [*pieces, normed, top, out, back],
        [ANY] * n + [VM] * 4,
        [shape(2 * LEN, d, dtype=BF16), *plan.piece_shapes(total)],
        [VM] + [ANY] * n,
        [
            pltpu.VMEM((d, total), BF16),
            pltpu.VMEM((d, total), BF16),
            pltpu.SemaphoreType.DMA((plan.n_copies(),)),
        ],
        2 * LEN * d * 9 * units,
    )


def cross_backward(
    plan, pieces, after_cross, top, sums_mine, sums_other, gain, normed, query, kv, probs, mixed, e_mine, e_other
):
    n = plan.pieces
    d = normed.shape[1]
    width = query.shape[1]
    pairs = width // (2 * DH)
    half_rows = LEN // 2

    def body(*refs):
        weights = refs[:n]
        after, top_ref, sm, so, g, normed_ref, q_ref, kv_ref, probs_ref, mixed_ref, em, eo = refs[n : n + 12]
        total_ref, sums, layer_out, grad_gain = refs[n + 12 : n + 16]
        grads_out = refs[n + 16 : 2 * n + 16]
        whole, grads, grad_q, grad_kv, sems = refs[2 * n + 16 :]
        copies = bring(plan, weights, whole, sems)
        core = lax.axis_index("tensor")
        back, gain_row = norm_back(after[...], g[...], wide_sum(sm.at[:LEN], so.at[:LEN]))
        grad_gain[...] = gain_row
        total = top_ref[...].astype(F32) + back
        total_ref[...] = total
        upstream = total.astype(BF16)
        first = pl.multiple_of(core * half_rows, half_rows)
        tail = pl.ds(pl.multiple_of(LEN + core * half_rows, half_rows), half_rows)
        layer_out[...] = (
            after[pl.ds(first, half_rows), :] + sm[tail, :].astype(F32) + so[tail, :].astype(F32)
        ).astype(BF16)
        states = rows_of(em[...], eo[...], core)
        finish(copies)
        grad_mixed = product(upstream, whole[:, 3 * width :]).astype(BF16)
        for pair in range(pairs):
            lanes = slice(pair * 128, (pair + 1) * 128)
            lanes_v = slice(width + pair * 128, width + (pair + 1) * 128)
            gq, gk, gv, _ = attend_back(
                q_ref[:, lanes],
                kv_ref[:, lanes],
                kv_ref[:, lanes_v],
                probs_ref[pl.ds(pair * 2 * LEN, 2 * LEN), :],
                grad_mixed[:, lanes],
            )
            grad_q[:, lanes] = gq
            grad_kv[:, lanes] = gk
            grad_kv[:, lanes_v] = gv
        sums[:LEN, :] = product_nt(grad_q[...], whole[:, :width]).astype(BF16)
        sums[LEN:, :] = product_nt(grad_kv[...], whole[:, width : 3 * width]).astype(BF16)
        grads[:, :width] = product_tn(normed_ref[...], grad_q[...]).astype(BF16)
        grads[:, width : 3 * width] = product_tn(states, grad_kv[...]).astype(BF16)
        grads[:, 3 * width :] = product_tn(upstream, mixed_ref[...]).astype(BF16)
        hand_out(plan, grads_out, grads, sems)

    return call(
        body,
        "cross_backward",
        [*pieces, after_cross, top, sums_mine, sums_other, gain, normed, query, kv, probs, mixed, e_mine, e_other],
        [ANY] * n + [VM] * 12,
        [
            shape(LEN, d),
            shape(LEN + ENC, d, dtype=BF16),
            shape(half_rows, d, dtype=BF16),
            shape(1, d),
            *plan.piece_shapes(4 * width),
        ],
        [VM] * 4 + [ANY] * n,
        [
            pltpu.VMEM((d, 4 * width), BF16),
            pltpu.VMEM((d, 4 * width), BF16),
            pltpu.VMEM((LEN, width), BF16),
            pltpu.VMEM((ENC, 2 * width), BF16),
            pltpu.SemaphoreType.DMA((plan.n_copies(),)),
        ],
        2 * LEN * d * 6 * width + 10 * LEN * ENC * width,
    )


def table_rows(per_distance, buckets, core, d):
    heads = len(per_distance)
    rows = jnp.concatenate(per_distance + [jnp.zeros_like(per_distance[0])] * (8 - heads), axis=0)
    lane = lax.broadcasted_iota(jnp.int32, (d, LEN), 0)
    table = exact_nt(rows, ((lane & (NB - 1)) == buckets).astype(F32))
    lane = lax.broadcasted_iota(jnp.int32, (8, d), 1)
    head = lax.broadcasted_iota(jnp.int32, (8, d), 0)
    kept = ((lane >> 5) == head + core * heads) & (head < heads)
    row = jnp.sum(jnp.where(kept, table, 0.0), axis=0, keepdims=True)
    high = row.astype(BF16)
    low = (row - high.astype(F32)).astype(BF16)
    return jnp.concatenate([high, low, jnp.zeros((14, d), BF16)], axis=0)


def self_backward(
    plan, pieces, total_cross, after_self, sums_mine, sums_other, gain, normed, qkv, probs, mixed, buckets
):
    n = plan.pieces
    d = normed.shape[1]
    width = mixed.shape[1]
    pairs = width // (2 * DH)
    half_enc = ENC // 2

    def body(*refs):
        weights = refs[:n]
        tc, after, sm, so, g, normed_ref, qkv_ref, probs_ref, mixed_ref, buck = refs[n : n + 10]
        total_ref, sums, states_out, grad_gain = refs[n + 10 : n + 14]
        grads_out = refs[n + 14 : 2 * n + 14]
        whole, grads, grad_qkv, sems = refs[2 * n + 14 :]
        copies = bring(plan, weights, whole, sems, True)
        core = lax.axis_index("tensor")
        back, gain_row = norm_back(after[...], g[...], wide_sum(sm.at[:LEN], so.at[:LEN]))
        grad_gain[...] = gain_row
        total = tc[...] + back
        total_ref[...] = total
        upstream = total.astype(BF16)
        tail = pl.ds(pl.multiple_of(LEN + core * half_enc, half_enc), half_enc)
        states_out[...] = sm[tail, :].astype(F32) + so[tail, :].astype(F32)
        finish(copies)
        grad_mixed = product(upstream, whole[:, 3 * width :]).astype(BF16)
        backwards = reversal()
        per_distance = []
        for pair in range(pairs):
            lanes = slice(pair * 128, (pair + 1) * 128)
            lanes_k = slice(width + pair * 128, width + (pair + 1) * 128)
            lanes_v = slice(2 * width + pair * 128, 2 * width + (pair + 1) * 128)
            gq, gk, gv, gs = attend_back(
                qkv_ref[:, lanes],
                qkv_ref[:, lanes_k],
                qkv_ref[:, lanes_v],
                probs_ref[pl.ds(pair * 2 * LEN, 2 * LEN), :],
                grad_mixed[:, lanes],
            )
            grad_qkv[:, lanes] = gq
            grad_qkv[:, lanes_k] = gk
            grad_qkv[:, lanes_v] = gv
            turned_scores = product(gs, backwards)
            for h in range(2):
                rolled = pltpu.roll(
                    turned_scores[h * LEN : (h + 1) * LEN], 0, 1, stride=1, stride_axis=0
                )
                per_distance.append(jnp.sum(rolled, axis=0, keepdims=True))
        sums[:LEN, :] = product_nt(grad_qkv[...], whole[:, : 3 * width]).astype(BF16)
        sums[LEN:, :] = table_rows(per_distance, buck[...], core, d)
        grads[:, : 3 * width] = product_tn(normed_ref[...], grad_qkv[...]).astype(BF16)
        grads[:, 3 * width :] = product_tn(upstream, mixed_ref[...]).astype(BF16)
        hand_out(plan, grads_out, grads, sems, True)

    return call(
        body,
        "self_backward",
        [*pieces, total_cross, after_self, sums_mine, sums_other, gain, normed, qkv, probs, mixed, buckets],
        [ANY] * n + [VM] * 10,
        [
            shape(LEN, d),
            shape(LEN + 16, d, dtype=BF16),
            shape(half_enc, d),
            shape(1, d),
            *plan.piece_shapes(4 * width),
        ],
        [VM] * 4 + [ANY] * n,
        [
            pltpu.VMEM((d, 4 * width), BF16),
            pltpu.VMEM((d, 4 * width), BF16),
            pltpu.VMEM((LEN, 3 * width), BF16),
            pltpu.SemaphoreType.DMA((plan.n_copies(),)),
        ],
        2 * LEN * d * 8 * width + 14 * LEN * LEN * width,
    )


def last_norm(total_self, x_mine, x_other, sums_mine, sums_other, gain, gain_cross_row, gain_feed_row):
    d = total_self.shape[1]
    half_rows = LEN // 2

    def body(total, xm, xo, sm, so, g, ggc, ggf, grad_in, small):
        core = lax.axis_index("tensor")
        x = rows_of(xm[...], xo[...], core).astype(F32)
        back, gain_row = norm_back(x, g[...], wide_sum(sm.at[:LEN], so.at[:LEN]))
        whole = total[...] + back
        grad_in[...] = jnp.where(core == 0, whole[:half_rows], whole[half_rows:])
        table = jnp.sum(wide_sum(sm.at[LEN:], so.at[LEN:]), axis=0, keepdims=True)
        for number, row in enumerate((gain_row, ggc[...], ggf[...], table)):
            small[number : number + 1, :] = row[:, : d // 2]
            small[4 + number : 5 + number, :] = row[:, d // 2 :]

    return call(
        body,
        "last_norm",
        [total_self, x_mine, x_other, sums_mine, sums_other, gain, gain_cross_row, gain_feed_row],
        [VM] * 8,
        [shape(half_rows, d), shape(8, d // 2)],
        [VM] * 2,
        [],
        1 << 24,
    )


def shards(
    mesh,
    layer_in,
    enc_states,
    cotangent,
    gain_self,
    gain_cross,
    gain_feed,
    bias_table,
    self_query,
    self_key,
    self_value,
    self_out,
    cross_query,
    cross_key,
    cross_value,
    cross_out,
    gate_proj,
    up_proj,
    down_proj,
    dec_lengths,
    enc_lengths,
    seq_owner,
    bucket_table,
):
    plan = Plan(mesh, self_query.shape[0])
    d = layer_in.shape[1]
    width = self_query.shape[1]
    units = gate_proj.shape[1] // 2
    g_self, g_cross, g_feed = (g.reshape(1, d) for g in (gain_self, gain_cross, gain_feed))

    def attention_group(query, key, value, out):
        return [(m, 0, width) for m in (query, key, value, out.T)]

    def feed_group(number):
        return [(m, number * units, units) for m in (gate_proj, up_proj, down_proj.T)]

    (block_s,) = pack("pack_self", [attention_group(self_query, self_key, self_value, self_out)])
    block_c, block_f1, block_f2 = pack(
        "pack_rest",
        [attention_group(cross_query, cross_key, cross_value, cross_out), feed_group(0), feed_group(1)],
    )
    x_other = other_core(layer_in)
    e_other = other_core(enc_states)
    c_other = other_core(cotangent)
    buckets = jnp.concatenate([bucket_table[:1], bucket_table[:0:-1]]).reshape(1, LEN)
    buckets_up = jnp.concatenate([bucket_table[1:], bucket_table[:1]]).reshape(1, LEN)

    at_s = Gather(plan, block_s, direct=True)
    at_c = Gather(plan, block_c, x_other, e_other, c_other)
    at_s.near(block_c)
    at_c.line(*at_s.ready())
    at_s.far()
    at_f1 = Gather(plan, block_f1, *at_s.ready())
    at_c.near(*at_s.ready())
    at_f1.line(*at_c.ready())
    at_c.far()
    at_f2 = Gather(plan, block_f2, *at_c.ready())
    at_f1.near(*at_c.ready())
    part_s, normed_s, qkv, probs_s, mixed_s = self_forward(
        plan, at_s.pieces(), layer_in, after(x_other, *at_f1.ready()), g_self, bias_table.T, buckets, dec_lengths,
        seq_owner,
    )
    part_other = other_core(part_s)
    at_f2.line(part_s)
    at_f1.far(part_s)
    at_f2.near(*at_f1.ready())
    part_c, after_self, normed_c, cq, ckv, probs_c, mixed_c = cross_forward(
        plan, at_c.pieces(), layer_in, x_other, part_s, after(part_other, *at_f2.ready()), g_cross, enc_states,
        e_other, enc_lengths, seq_owner,
    )
    part_other = other_core(part_c)
    at_f2.far()
    after_cross, normed_f, top, out, back, *grads_f1 = feed_first(
        plan, at_f1.pieces(), after_self, part_c, after(part_other, *at_f2.ready()), g_feed, cotangent, c_other,
        dec_lengths, seq_owner,
    )
    sum_f1 = Scatter(plan, grads_f1)
    sums_f, *grads_f2 = feed_second(plan, at_f2.pieces(), normed_f, top, out, back)
    sum_f1.near(sums_f)
    sum_f2 = Scatter(plan, grads_f2)
    total_cross, sums_c, layer_out, gain_feed_row, *grads_c = cross_backward(
        plan, at_c.pieces(), after_cross, top, sums_f, after(other_core(sums_f), *sum_f1.ready()), g_feed, normed_c,
        cq, ckv, probs_c, mixed_c, enc_states, e_other,
    )
    sum_f1.line(sums_c)
    sum_f2.near(sums_c)
    sum_c = Scatter(plan, grads_c)
    total_self, sums_s, grad_states, gain_cross_row, *grads_s = self_backward(
        plan, at_s.pieces(), total_cross, after_self, sums_c, after(other_core(sums_c), *sum_f2.ready()), g_cross,
        normed_s, qkv, probs_s, mixed_s, buckets_up,
    )
    sum_c.near(sums_s)
    sum_s = Scatter(plan, grads_s, *(sum_c.gots if plan.staged else ()))
    sums_other = other_core(sums_s)
    sum_f1.last(sums_s)
    grad_in, small = last_norm(
        total_self, layer_in, x_other, sums_s, after(sums_other, *sum_c.ready()), g_self, gain_cross_row,
        gain_feed_row,
    )
    sum_f2.line(sums_s)
    sum_f2.last()
    sum_c.line()
    sum_c.last()
    sum_s.near(small)
    sum_s.direct()
    line_s = sum_s.ready()
    grad_f1 = sum_f1.total(*line_s)
    grad_f2 = sum_f2.total(*line_s)
    grad_c = sum_c.total(*line_s)
    grad_s = sum_s.total()
    small = sum_everywhere(plan, small, line_s)
    small = jnp.concatenate([small[:4], small[4:]], axis=1)
    table_grad = small[3, : H * NB].reshape(H, NB).T

    def columns(block, number, size):
        return block[:, number * size : (number + 1) * size]

    def feed(number):
        return jnp.concatenate([columns(g, number, units) for g in (grad_f1, grad_f2)], axis=1)

    return (
        layer_out,
        grad_in,
        grad_states,
        small[0],
        small[1],
        small[2],
        table_grad,
        columns(grad_s, 0, width),
        columns(grad_s, 1, width),
        columns(grad_s, 2, width),
        columns(grad_s, 3, width).T,
        columns(grad_c, 0, width),
        columns(grad_c, 1, width),
        columns(grad_c, 2, width),
        columns(grad_c, 3, width).T,
        feed(0),
        feed(1),
        feed(2).T,
    )


def solution(mesh):
    rows = P(("dp", "tensor"), None)
    into, out = P("dp", "tensor"), P("tensor", "dp")
    weights = (into, into, into, out, into, into, into, out, into, into, out)
    in_specs = (rows, rows, rows, P(), P(), P(), P(), *weights, P(), P(), P(), P())
    out_specs = (rows, rows, rows, P(), P(), P(), P(), *weights)
    return jax.shard_map(
        functools.partial(shards, mesh), mesh=mesh, in_specs=in_specs, out_specs=out_specs, check_vma=False
    )
```

```python
import functools

import jax
import jax.numpy as jnp
from jax import lax
from jax.experimental import pallas as pl
from jax.experimental.pallas import tpu as pltpu
from jax.sharding import PartitionSpec as P

H = 12
DH = 64
NB = 32
LEN = 256
ENC = 128
EPSILON = 1e-06
NEGATIVE = -1e30
F32 = jnp.float32
BF16 = jnp.bfloat16
VMEM_LIMIT = 56 * 1024 * 1024


def product(left, right):
    return jnp.dot(left, right, preferred_element_type=F32)


def product_tn(left, right):
    return lax.dot_general(left, right, (((0,), (0,)), ((), ())), preferred_element_type=F32)


def product_nt(left, right):
    return lax.dot_general(left, right, (((1,), (1,)), ((), ())), preferred_element_type=F32)


def exact_nt(left, right):
    return lax.dot_general(
        left, right, (((1,), (1,)), ((), ())), preferred_element_type=F32, precision=lax.Precision.HIGHEST
    )


def inverse_rms(values):
    return lax.rsqrt(jnp.mean(values * values, axis=-1, keepdims=True) + EPSILON)


def norm_back(values, gain, upstream):
    inverse = inverse_rms(values)
    scaled = upstream * gain
    inner = jnp.mean(scaled * values, axis=-1, keepdims=True)
    grad_values = inverse * scaled - values * (inverse * inverse * inverse * inner)
    grad_gain = jnp.sum(upstream * values * inverse, axis=0, keepdims=True)
    return grad_values, grad_gain


def both_heads(pair):
    first = lax.broadcasted_iota(jnp.int32, pair.shape, 1) < DH
    zero = jnp.zeros_like(pair)
    return jnp.concatenate([jnp.where(first, pair, zero), jnp.where(first, zero, pair)], axis=0)


def join_heads(stacked):
    rows = stacked.shape[0] // 2
    first = lax.broadcasted_iota(jnp.int32, (rows, stacked.shape[1]), 1) < DH
    return jnp.where(first, stacked[:rows], stacked[rows:])


def softmax(scores):
    expo = jnp.exp(scores - jnp.max(scores, axis=-1, keepdims=True))
    return expo * (1.0 / jnp.sum(expo, axis=-1, keepdims=True))


def attend_back(query, keys, values, probs, upstream):
    upper = both_heads(upstream)
    grad_probs = product_nt(upper, values)
    inner = jnp.sum(probs * grad_probs, axis=-1, keepdims=True)
    grad_scores = (probs * (grad_probs - inner)).astype(BF16)
    grad_query = join_heads(product(grad_scores, keys)).astype(BF16)
    grad_keys = product_tn(grad_scores, both_heads(query)).astype(BF16)
    grad_values = product_tn(probs.astype(BF16), upper).astype(BF16)
    return grad_query, grad_keys, grad_values, grad_scores


def bucket_onehot(buckets):
    return (lax.broadcasted_iota(jnp.int32, (NB, LEN), 0) == buckets).astype(F32)


def reversal():
    shape = (LEN, LEN)
    return (
        lax.broadcasted_iota(jnp.int32, shape, 0) + lax.broadcasted_iota(jnp.int32, shape, 1) == LEN - 1
    ).astype(BF16)


class Plan:
    LINE = (0, 8, 4, 12)
    BITS = ((1, 2), (2, 1))

    def __init__(self, mesh, rows):
        self.size = mesh.shape["dp"]
        self.rows = rows
        self.staged = self.size == 16 and rows % 16 == 0
        self.pieces = 4 if self.staged else 1

    def line(self, here, direct):
        if direct:
            return [((here - 4 * step) & 12) | (here & 3) for step in range(4)]
        return [here ^ mask for mask in self.LINE]

    def spans(self, direct):
        if not self.staged:
            return [(0, 0, 0, self.size * self.rows, None)]
        here = lax.axis_index("dp")
        result = []
        for half, (first_bit, second_bit) in enumerate(self.BITS):
            for far in range(2):
                line = self.line(here ^ (far * second_bit), direct)
                for number, device in enumerate(line + [other ^ first_bit for other in line]):
                    first = pl.multiple_of(device * self.rows, 16)
                    result.append((2 * half + far, number * self.rows, first, self.rows, half))
        return result

    def copies(self, pieces, whole, sems, forward, direct):
        width = whole.shape[1] // 2
        result = []
        for number, (piece, row, first, rows, half) in enumerate(self.spans(direct)):
            columns = pl.ds(0, 2 * width) if half is None else pl.ds(half * width, width)
            part = pieces[piece].at[pl.ds(row, rows), :]
            block = whole.at[pl.ds(first, rows), columns]
            ends = (part, block) if forward else (block, part)
            result.append(pltpu.make_async_copy(*ends, sems.at[number]))
        return result

    def n_copies(self):
        return 32 if self.staged else 1

    def piece_shapes(self, width):
        if self.staged:
            return [jax.ShapeDtypeStruct((8 * self.rows, width // 2), BF16)] * 4
        return [jax.ShapeDtypeStruct((self.size * self.rows, width), BF16)]


def swap(block, axis_bit, size):
    return lax.ppermute(block, "dp", [(i, i ^ axis_bit) for i in range(size)])


def shift_z(block, step):
    return lax.ppermute(block, "dp", [(i, ((i + 4 * step) & 12) | (i & 3)) for i in range(16)])


def after(value, *events):
    return lax.optimization_barrier((value, *events))[0] if events else value


def wide(value):
    return value.astype(F32)


def stack(*blocks):
    return jnp.concatenate(blocks, axis=0)


class Gather:
    def __init__(self, plan, block, *events, direct=False):
        self.plan, self.direct = plan, direct
        block = after(block, *events)
        if plan.staged and direct:
            self.block, self.got = block, [shift_z(block, step) for step in (1, 2, 3)]
        elif plan.staged:
            self.block, self.got = block, swap(block, 8, 16)
        else:
            self.got = lax.all_gather(block, "dp", axis=0, tiled=True)

    def line(self, *events):
        if self.plan.staged:
            self.block = stack(self.block, after(self.got, *events))
            self.sent = [self.block]
            self.got = swap(self.block, 4, 16)

    def near(self, *events):
        if self.plan.staged:
            gots = self.got if self.direct else [self.got]
            whole = stack(self.block, *(after(got, *events) for got in gots))
            width = whole.shape[1] // 2
            self.sent = self.halves = [whole[:, :width], whole[:, width:]]
            self.gots = [swap(half, bits[0], 16) for half, bits in zip(self.halves, Plan.BITS)]
            self.got = self.gots[0]

    def far(self, *events):
        if self.plan.staged:
            self.sent = self.halves = [stack(half, after(got, *events)) for half, got in zip(self.halves, self.gots)]
            self.gots = [swap(half, bits[1], 16) for half, bits in zip(self.halves, Plan.BITS)]
            self.got = self.gots[0]

    def ready(self):
        return self.sent if self.plan.staged else []

    def pieces(self):
        if not self.plan.staged:
            return [self.got]
        return [self.halves[0], self.gots[0], self.halves[1], self.gots[1]]


class Scatter:
    def __init__(self, plan, pieces, *events):
        self.plan = plan
        if plan.staged:
            self.sums = [wide(pieces[0]), wide(pieces[2])]
            self.gots = [
                swap(after(piece, *events), bits[1], 16) for piece, bits in zip((pieces[1], pieces[3]), Plan.BITS)
            ]
            self.got = self.gots[0]
        else:
            self.got = lax.psum_scatter(wide(pieces[0]), "dp", scatter_dimension=0, tiled=True)

    def near(self, *events):
        if self.plan.staged:
            rows = 4 * self.plan.rows
            sums = [one + wide(after(got, *events)) for one, got in zip(self.sums, self.gots)]
            self.sent = [one[rows:].astype(BF16) for one in sums]
            self.gots = [swap(one, bits[0], 16) for one, bits in zip(self.sent, Plan.BITS)]
            self.sums = [one[:rows] for one in sums]
            self.got = self.gots[0]

    def line(self, *events):
        if self.plan.staged:
            rows = 2 * self.plan.rows
            whole = jnp.concatenate(
                [one + wide(after(got, *events)) for one, got in zip(self.sums, self.gots)], axis=1
            )
            self.sent = [whole[rows:].astype(BF16)]
            self.got = swap(self.sent[0], 4, 16)
            self.sums = whole[:rows]

    def direct(self, *events):
        if self.plan.staged:
            rows = self.plan.rows
            whole = jnp.concatenate(
                [one + wide(after(got, *events)) for one, got in zip(self.sums, self.gots)], axis=1
            )
            self.sent = [whole[step * rows : (step + 1) * rows].astype(BF16) for step in (1, 2, 3)]
            gots = [shift_z(one, -step) for step, one in zip((1, 2, 3), self.sent)]
            self.sums = whole[:rows] + wide(gots[0]) + wide(gots[1])
            self.got = gots[2]

    def last(self, *events):
        if self.plan.staged:
            rows = self.plan.rows
            whole = self.sums + wide(after(self.got, *events))
            self.sent = [whole[rows:].astype(BF16)]
            self.got = swap(self.sent[0], 8, 16)
            self.sums = whole[:rows]

    def ready(self):
        return self.sent if self.plan.staged else []

    def total(self, *events):
        if self.plan.staged:
            return self.sums + wide(after(self.got, *events))
        return self.got


def other_core(block):
    return lax.ppermute(block, "tensor", [(0, 1), (1, 0)])


def sum_everywhere(plan, block, events):
    if not plan.staged:
        return lax.psum(block, "dp")
    terms = lax.all_to_all(jnp.tile(block, (plan.size, 1)), "dp", 0, 0, tiled=True)
    terms = after(terms, *events)
    return jnp.sum(terms.reshape(plan.size, *block.shape), axis=0)


VM = pl.BlockSpec(memory_space=pltpu.VMEM)
SM = pl.BlockSpec(memory_space=pltpu.SMEM)
ANY = pl.BlockSpec(memory_space=pl.ANY)


def call(body, name, inputs, specs, outputs, out_specs, scratch, flops):
    nbytes = sum(a.size * a.dtype.itemsize for a in inputs) + sum(
        a.size * jnp.dtype(a.dtype).itemsize for a in outputs
    )
    return pl.pallas_call(
        body,
        name=name,
        out_shape=outputs,
        in_specs=specs,
        out_specs=out_specs,
        scratch_shapes=scratch,
        compiler_params=pltpu.CompilerParams(vmem_limit_bytes=VMEM_LIMIT),
        cost_estimate=pl.CostEstimate(flops=0, bytes_accessed=0, transcendentals=0),
    )(*inputs)


def shape(*dims, dtype=F32):
    return jax.ShapeDtypeStruct(dims, dtype)


def rows_of(mine, other, core):
    first = jnp.where(core == 0, mine, other)
    second = jnp.where(core == 0, other, mine)
    return jnp.concatenate([first, second], axis=0)


def wide_sum(mine, other):
    return mine[...].astype(F32) + other[...].astype(F32)


def pack(name, groups):
    arrays = [block[0] for group in groups for block in group]
    rows = arrays[0].shape[0]
    if rows % 16:
        return [jnp.concatenate([m[:, at : at + size] for m, at, size in group], axis=1) for group in groups]

    def body(*refs):
        ins, outs = list(refs[: len(arrays)]), refs[len(arrays) :]
        for group, out in zip(groups, outs):
            column = 0
            for _, at, size in group:
                out[:, column : column + size] = ins.pop(0)[:, at : at + size]
                column += size

    return pl.pallas_call(
        body,
        name=name,
        out_shape=[shape(rows, sum(block[2] for block in group), dtype=BF16) for group in groups],
        in_specs=[VM] * len(arrays),
        out_specs=[VM] * len(groups),
        compiler_params=pltpu.CompilerParams(vmem_limit_bytes=VMEM_LIMIT),
    )(*arrays)


def bring(plan, pieces, whole, sems, direct=False):
    copies = plan.copies(pieces, whole, sems, True, direct)
    for copy in copies:
        copy.start()
    return copies


def finish(copies):
    for copy in copies:
        copy.wait()


def hand_out(plan, pieces, whole, sems, direct=False):
    copies = plan.copies(pieces, whole, sems, False, direct)
    for copy in copies:
        copy.start()
    finish(copies)


def self_forward(plan, pieces, x_mine, x_other, gain, table, buckets, dec_lengths, owner):
    n = plan.pieces
    d = x_mine.shape[1]
    width = pieces[0].shape[1] // (2 if plan.staged else 4)
    pairs = width // (2 * DH)

    def body(*refs):
        weights = refs[:n]
        xm, xo, g, tab, buck, lens, own = refs[n : n + 7]
        part, normed_ref, qkv, probs_ref, mixed_ref, whole, sems = refs[n + 7 :]
        copies = bring(plan, weights, whole, sems, True)
        core = lax.axis_index("tensor")
        length = lens[own[lax.axis_index("dp")]]
        x = rows_of(xm[...], xo[...], core).astype(F32)
        normed = (x * inverse_rms(x) * g[...]).astype(BF16)
        normed_ref[...] = normed
        distances = lax.dot_general(
            tab[...], bucket_onehot(buck[...]), (((1,), (0,)), ((), ())),
            preferred_element_type=F32, precision=lax.Precision.HIGHEST,
        )
        heads = 2 * pairs
        mine = distances[:heads]
        for other in range(1, H // heads):
            mine = jnp.where(core == other, distances[other * heads : (other + 1) * heads], mine)
        row = lax.broadcasted_iota(jnp.int32, (2 * LEN, LEN), 0) & (LEN - 1)
        key = lax.broadcasted_iota(jnp.int32, (2 * LEN, LEN), 1)
        allowed = (key <= row) & (key < length)
        finish(copies)
        qkv[...] = product(normed, whole[:, : 3 * width]).astype(BF16)
        for pair in range(pairs):
            lanes = slice(pair * 128, (pair + 1) * 128)
            query = qkv[:, lanes]
            keys = qkv[:, width + pair * 128 : width + (pair + 1) * 128]
            values = qkv[:, 2 * width + pair * 128 : 2 * width + (pair + 1) * 128]
            extra = jnp.concatenate(
                [
                    pltpu.roll(
                        jnp.broadcast_to(mine[h : h + 1], (LEN, LEN)), 0, 1, stride=1, stride_axis=0
                    )
                    for h in (2 * pair, 2 * pair + 1)
                ],
                axis=0,
            )
            scores = product_nt(both_heads(query), keys) + extra
            probs = softmax(jnp.where(allowed, scores, NEGATIVE))
            probs_ref[pl.ds(pair * 2 * LEN, 2 * LEN), :] = probs
            mixed_ref[:, lanes] = join_heads(product(probs.astype(BF16), values)).astype(BF16)
        part[...] = product_nt(mixed_ref[...], whole[:, 3 * width :]).astype(BF16)

    outputs = [
        shape(LEN, d, dtype=BF16),
        shape(LEN, d, dtype=BF16),
        shape(LEN, 3 * width, dtype=BF16),
        shape(pairs * 2 * LEN, LEN),
        shape(LEN, width, dtype=BF16),
    ]
    return call(
        body,
        "self_forward",
        [*pieces, x_mine, x_other, gain, table, buckets, dec_lengths, owner],
        [ANY] * n + [VM] * 5 + [SM] * 2,
        outputs,
        [VM] * 5,
        [pltpu.VMEM((d, 4 * width), BF16), pltpu.SemaphoreType.DMA((plan.n_copies(),))],
        2 * LEN * d * 4 * width + 8 * LEN * LEN * width,
    )


def cross_forward(plan, pieces, x_mine, x_other, part_mine, part_other, gain, e_mine, e_other, enc_lengths, owner):
    n = plan.pieces
    d = x_mine.shape[1]
    width = pieces[0].shape[1] // (2 if plan.staged else 4)
    pairs = width // (2 * DH)

    def body(*refs):
        weights = refs[:n]
        xm, xo, pm, po, g, em, eo, lens, own = refs[n : n + 9]
        part, after_ref, normed_ref, q_ref, kv, probs_ref, mixed_ref, whole, sems = refs[n + 9 :]
        copies = bring(plan, weights, whole, sems)
        core = lax.axis_index("tensor")
        length = lens[own[lax.axis_index("dp")]]
        after = rows_of(xm[...], xo[...], core).astype(F32) + wide_sum(pm, po)
        after_ref[...] = after
        normed = (after * inverse_rms(after) * g[...]).astype(BF16)
        normed_ref[...] = normed
        allowed = lax.broadcasted_iota(jnp.int32, (2 * LEN, ENC), 1) < length
        finish(copies)
        kv[...] = product(rows_of(em[...], eo[...], core), whole[:, width : 3 * width]).astype(BF16)
        q_ref[...] = product(normed, whole[:, :width]).astype(BF16)
        for pair in range(pairs):
            lanes = slice(pair * 128, (pair + 1) * 128)
            keys = kv[:, lanes]
            values = kv[:, width + pair * 128 : width + (pair + 1) * 128]
            scores = product_nt(both_heads(q_ref[:, lanes]), keys)
            probs = softmax(jnp.where(allowed, scores, NEGATIVE))
            probs_ref[pl.ds(pair * 2 * LEN, 2 * LEN), :] = probs
            mixed_ref[:, lanes] = join_heads(product(probs.astype(BF16), values)).astype(BF16)
        part[...] = product_nt(mixed_ref[...], whole[:, 3 * width :]).astype(BF16)

    outputs = [
        shape(LEN, d, dtype=BF16),
        shape(LEN, d),
        shape(LEN, d, dtype=BF16),
        shape(LEN, width, dtype=BF16),
        shape(ENC, 2 * width, dtype=BF16),
        shape(pairs * 2 * LEN, ENC),
        shape(LEN, width, dtype=BF16),
    ]
    return call(
        body,
        "cross_forward",
        [*pieces, x_mine, x_other, part_mine, part_other, gain, e_mine, e_other, enc_lengths, owner],
        [ANY] * n + [VM] * 7 + [SM] * 2,
        outputs,
        [VM] * 7,
        [pltpu.VMEM((d, 4 * width), BF16), pltpu.SemaphoreType.DMA((plan.n_copies(),))],
        2 * LEN * d * 3 * width + 4 * LEN * ENC * width,
    )


GELU_C = 0.7978845608028654


def feed_units(normed, top, whole, grads, units):
    gate = product(normed, whole[:, :units])
    upper = product(normed, whole[:, units : 2 * units])
    square = gate * gate
    tanh = jnp.tanh(GELU_C * gate * (1.0 + 0.044715 * square))
    half = 0.5 * (1.0 + tanh)
    gelu = gate * half
    slope = half + 0.5 * gate * (1.0 - tanh * tanh) * (GELU_C * (1.0 + 3 * 0.044715 * square))
    hidden = (gelu * upper).astype(BF16)
    grad_hidden = product(top, whole[:, 2 * units :])
    grad_gate = (grad_hidden * upper * slope).astype(BF16)
    grad_up = (grad_hidden * gelu).astype(BF16)
    out = product_nt(hidden, whole[:, 2 * units :])
    back = product_nt(grad_gate, whole[:, :units]) + product_nt(grad_up, whole[:, units : 2 * units])
    grads[:, :units] = product_tn(normed, grad_gate).astype(BF16)
    grads[:, units : 2 * units] = product_tn(normed, grad_up).astype(BF16)
    grads[:, 2 * units :] = product_tn(top, hidden).astype(BF16)
    return out, back


def feed_first(plan, pieces, after_self, part_mine, part_other, gain, c_mine, c_other, dec_lengths, owner):
    n = plan.pieces
    d = after_self.shape[1]
    total = pieces[0].shape[1] * (2 if plan.staged else 1)
    units = total // 3

    def body(*refs):
        weights = refs[:n]
        a_ref, pm, po, g, cm, co, lens, own = refs[n : n + 8]
        after_ref, normed_ref, top_ref, out_ref, back_ref = refs[n + 8 : n + 13]
        grads_out = refs[n + 13 : 2 * n + 13]
        whole, grads, sems = refs[2 * n + 13 :]
        copies = bring(plan, weights, whole, sems)
        core = lax.axis_index("tensor")
        length = lens[own[lax.axis_index("dp")]]
        after = a_ref[...] + wide_sum(pm, po)
        after_ref[...] = after
        normed = (after * inverse_rms(after) * g[...]).astype(BF16)
        normed_ref[...] = normed
        cot = rows_of(cm[...], co[...], core)
        valid = lax.broadcasted_iota(jnp.int32, cot.shape, 0) < length
        top = jnp.where(valid, cot.astype(F32), 0.0).astype(BF16)
        top_ref[...] = top
        finish(copies)
        out_ref[...], back_ref[...] = feed_units(normed, top, whole, grads, units)
        hand_out(plan, grads_out, grads, sems)

    outputs = [
        shape(LEN, d),
        shape(LEN, d, dtype=BF16),
        shape(LEN, d, dtype=BF16),
        shape(LEN, d),
        shape(LEN, d),
        *plan.piece_shapes(total),
    ]
    return call(
        body,
        "feed_first",
        [*pieces, after_self, part_mine, part_other, gain, c_mine, c_other, dec_lengths, owner],
        [ANY] * n + [VM] * 6 + [SM] * 2,
        outputs,
        [VM] * 5 + [ANY] * n,
        [
            pltpu.VMEM((d, total), BF16),
            pltpu.VMEM((d, total), BF16),
            pltpu.SemaphoreType.DMA((plan.n_copies(),)),
        ],
        2 * LEN * d * 9 * units,
    )


def feed_second(plan, pieces, normed, top, out, back):
    n = plan.pieces
    d = normed.shape[1]
    total = pieces[0].shape[1] * (2 if plan.staged else 1)
    units = total // 3

    def body(*refs):
        weights = refs[:n]
        normed_ref, top_ref, out_ref, back_ref = refs[n : n + 4]
        sums = refs[n + 4]
        grads_out = refs[n + 5 : 2 * n + 5]
        whole, grads, sems = refs[2 * n + 5 :]
        copies = bring(plan, weights, whole, sems)
        finish(copies)
        more_out, more_back = feed_units(normed_ref[...], top_ref[...], whole, grads, units)
        sums[:LEN, :] = (back_ref[...] + more_back).astype(BF16)
        sums[LEN:, :] = (out_ref[...] + more_out).astype(BF16)
        hand_out(plan, grads_out, grads, sems)

    return call(
        body,
        "feed_second",
        [*pieces, normed, top, out, back],
        [ANY] * n + [VM] * 4,
        [shape(2 * LEN, d, dtype=BF16), *plan.piece_shapes(total)],
        [VM] + [ANY] * n,
        [
            pltpu.VMEM((d, total), BF16),
            pltpu.VMEM((d, total), BF16),
            pltpu.SemaphoreType.DMA((plan.n_copies(),)),
        ],
        2 * LEN * d * 9 * units,
    )


def cross_backward(
    plan, pieces, after_cross, top, sums_mine, sums_other, gain, normed, query, kv, probs, mixed, e_mine, e_other
):
    n = plan.pieces
    d = normed.shape[1]
    width = query.shape[1]
    pairs = width // (2 * DH)
    half_rows = LEN // 2

    def body(*refs):
        weights = refs[:n]
        after, top_ref, sm, so, g, normed_ref, q_ref, kv_ref, probs_ref, mixed_ref, em, eo = refs[n : n + 12]
        total_ref, sums, layer_out, grad_gain = refs[n + 12 : n + 16]
        grads_out = refs[n + 16 : 2 * n + 16]
        whole, grads, grad_q, grad_kv, sems = refs[2 * n + 16 :]
        copies = bring(plan, weights, whole, sems)
        core = lax.axis_index("tensor")
        back, gain_row = norm_back(after[...], g[...], wide_sum(sm.at[:LEN], so.at[:LEN]))
        grad_gain[...] = gain_row
        total = top_ref[...].astype(F32) + back
        total_ref[...] = total
        upstream = total.astype(BF16)
        first = pl.multiple_of(core * half_rows, half_rows)
        tail = pl.ds(pl.multiple_of(LEN + core * half_rows, half_rows), half_rows)
        layer_out[...] = (
            after[pl.ds(first, half_rows), :] + sm[tail, :].astype(F32) + so[tail, :].astype(F32)
        ).astype(BF16)
        states = rows_of(em[...], eo[...], core)
        finish(copies)
        grad_mixed = product(upstream, whole[:, 3 * width :]).astype(BF16)
        for pair in range(pairs):
            lanes = slice(pair * 128, (pair + 1) * 128)
            lanes_v = slice(width + pair * 128, width + (pair + 1) * 128)
            gq, gk, gv, _ = attend_back(
                q_ref[:, lanes],
                kv_ref[:, lanes],
                kv_ref[:, lanes_v],
                probs_ref[pl.ds(pair * 2 * LEN, 2 * LEN), :],
                grad_mixed[:, lanes],
            )
            grad_q[:, lanes] = gq
            grad_kv[:, lanes] = gk
            grad_kv[:, lanes_v] = gv
        sums[:LEN, :] = product_nt(grad_q[...], whole[:, :width]).astype(BF16)
        sums[LEN:, :] = product_nt(grad_kv[...], whole[:, width : 3 * width]).astype(BF16)
        grads[:, :width] = product_tn(normed_ref[...], grad_q[...]).astype(BF16)
        grads[:, width : 3 * width] = product_tn(states, grad_kv[...]).astype(BF16)
        grads[:, 3 * width :] = product_tn(upstream, mixed_ref[...]).astype(BF16)
        hand_out(plan, grads_out, grads, sems)

    return call(
        body,
        "cross_backward",
        [*pieces, after_cross, top, sums_mine, sums_other, gain, normed, query, kv, probs, mixed, e_mine, e_other],
        [ANY] * n + [VM] * 12,
        [
            shape(LEN, d),
            shape(LEN + ENC, d, dtype=BF16),
            shape(half_rows, d, dtype=BF16),
            shape(1, d),
            *plan.piece_shapes(4 * width),
        ],
        [VM] * 4 + [ANY] * n,
        [
            pltpu.VMEM((d, 4 * width), BF16),
            pltpu.VMEM((d, 4 * width), BF16),
            pltpu.VMEM((LEN, width), BF16),
            pltpu.VMEM((ENC, 2 * width), BF16),
            pltpu.SemaphoreType.DMA((plan.n_copies(),)),
        ],
        2 * LEN * d * 6 * width + 10 * LEN * ENC * width,
    )


def table_rows(per_distance, buckets, core, d):
    heads = len(per_distance)
    rows = jnp.concatenate(per_distance + [jnp.zeros_like(per_distance[0])] * (8 - heads), axis=0)
    lane = lax.broadcasted_iota(jnp.int32, (d, LEN), 0)
    table = exact_nt(rows, ((lane & (NB - 1)) == buckets).astype(F32))
    lane = lax.broadcasted_iota(jnp.int32, (8, d), 1)
    head = lax.broadcasted_iota(jnp.int32, (8, d), 0)
    kept = ((lane >> 5) == head + core * heads) & (head < heads)
    row = jnp.sum(jnp.where(kept, table, 0.0), axis=0, keepdims=True)
    high = row.astype(BF16)
    low = (row - high.astype(F32)).astype(BF16)
    return jnp.concatenate([high, low, jnp.zeros((14, d), BF16)], axis=0)


def self_backward(
    plan, pieces, total_cross, after_self, sums_mine, sums_other, gain, normed, qkv, probs, mixed, buckets
):
    n = plan.pieces
    d = normed.shape[1]
    width = mixed.shape[1]
    pairs = width // (2 * DH)
    half_enc = ENC // 2

    def body(*refs):
        weights = refs[:n]
        tc, after, sm, so, g, normed_ref, qkv_ref, probs_ref, mixed_ref, buck = refs[n : n + 10]
        total_ref, sums, states_out, grad_gain = refs[n + 10 : n + 14]
        grads_out = refs[n + 14 : 2 * n + 14]
        whole, grads, grad_qkv, sems = refs[2 * n + 14 :]
        copies = bring(plan, weights, whole, sems, True)
        core = lax.axis_index("tensor")
        back, gain_row = norm_back(after[...], g[...], wide_sum(sm.at[:LEN], so.at[:LEN]))
        grad_gain[...] = gain_row
        total = tc[...] + back
        total_ref[...] = total
        upstream = total.astype(BF16)
        tail = pl.ds(pl.multiple_of(LEN + core * half_enc, half_enc), half_enc)
        states_out[...] = sm[tail, :].astype(F32) + so[tail, :].astype(F32)
        finish(copies)
        grad_mixed = product(upstream, whole[:, 3 * width :]).astype(BF16)
        backwards = reversal()
        per_distance = []
        for pair in range(pairs):
            lanes = slice(pair * 128, (pair + 1) * 128)
            lanes_k = slice(width + pair * 128, width + (pair + 1) * 128)
            lanes_v = slice(2 * width + pair * 128, 2 * width + (pair + 1) * 128)
            gq, gk, gv, gs = attend_back(
                qkv_ref[:, lanes],
                qkv_ref[:, lanes_k],
                qkv_ref[:, lanes_v],
                probs_ref[pl.ds(pair * 2 * LEN, 2 * LEN), :],
                grad_mixed[:, lanes],
            )
            grad_qkv[:, lanes] = gq
            grad_qkv[:, lanes_k] = gk
            grad_qkv[:, lanes_v] = gv
            turned_scores = product(gs, backwards)
            for h in range(2):
                rolled = pltpu.roll(
                    turned_scores[h * LEN : (h + 1) * LEN], 0, 1, stride=1, stride_axis=0
                )
                per_distance.append(jnp.sum(rolled, axis=0, keepdims=True))
        sums[:LEN, :] = product_nt(grad_qkv[...], whole[:, : 3 * width]).astype(BF16)
        sums[LEN:, :] = table_rows(per_distance, buck[...], core, d)
        grads[:, : 3 * width] = product_tn(normed_ref[...], grad_qkv[...]).astype(BF16)
        grads[:, 3 * width :] = product_tn(upstream, mixed_ref[...]).astype(BF16)
        hand_out(plan, grads_out, grads, sems, True)

    return call(
        body,
        "self_backward",
        [*pieces, total_cross, after_self, sums_mine, sums_other, gain, normed, qkv, probs, mixed, buckets],
        [ANY] * n + [VM] * 10,
        [
            shape(LEN, d),
            shape(LEN + 16, d, dtype=BF16),
            shape(half_enc, d),
            shape(1, d),
            *plan.piece_shapes(4 * width),
        ],
        [VM] * 4 + [ANY] * n,
        [
            pltpu.VMEM((d, 4 * width), BF16),
            pltpu.VMEM((d, 4 * width), BF16),
            pltpu.VMEM((LEN, 3 * width), BF16),
            pltpu.SemaphoreType.DMA((plan.n_copies(),)),
        ],
        2 * LEN * d * 8 * width + 14 * LEN * LEN * width,
    )


def last_norm(total_self, x_mine, x_other, sums_mine, sums_other, gain, gain_cross_row, gain_feed_row):
    d = total_self.shape[1]
    half_rows = LEN // 2

    def body(total, xm, xo, sm, so, g, ggc, ggf, grad_in, small):
        core = lax.axis_index("tensor")
        x = rows_of(xm[...], xo[...], core).astype(F32)
        back, gain_row = norm_back(x, g[...], wide_sum(sm.at[:LEN], so.at[:LEN]))
        whole = total[...] + back
        grad_in[...] = jnp.where(core == 0, whole[:half_rows], whole[half_rows:])
        table = jnp.sum(wide_sum(sm.at[LEN:], so.at[LEN:]), axis=0, keepdims=True)
        for number, row in enumerate((gain_row, ggc[...], ggf[...], table)):
            small[number : number + 1, :] = row[:, : d // 2]
            small[4 + number : 5 + number, :] = row[:, d // 2 :]

    return call(
        body,
        "last_norm",
        [total_self, x_mine, x_other, sums_mine, sums_other, gain, gain_cross_row, gain_feed_row],
        [VM] * 8,
        [shape(half_rows, d), shape(8, d // 2)],
        [VM] * 2,
        [],
        1 << 24,
    )


def shards(
    mesh,
    layer_in,
    enc_states,
    cotangent,
    gain_self,
    gain_cross,
    gain_feed,
    bias_table,
    self_query,
    self_key,
    self_value,
    self_out,
    cross_query,
    cross_key,
    cross_value,
    cross_out,
    gate_proj,
    up_proj,
    down_proj,
    dec_lengths,
    enc_lengths,
    seq_owner,
    bucket_table,
):
    plan = Plan(mesh, self_query.shape[0])
    d = layer_in.shape[1]
    width = self_query.shape[1]
    units = gate_proj.shape[1] // 2
    g_self, g_cross, g_feed = (g.reshape(1, d) for g in (gain_self, gain_cross, gain_feed))

    def attention_group(query, key, value, out):
        return [(m, 0, width) for m in (query, key, value, out.T)]

    def feed_group(number):
        return [(m, number * units, units) for m in (gate_proj, up_proj, down_proj.T)]

    (block_s,) = pack("pack_self", [attention_group(self_query, self_key, self_value, self_out)])
    block_c, block_f1, block_f2 = pack(
        "pack_rest",
        [attention_group(cross_query, cross_key, cross_value, cross_out), feed_group(0), feed_group(1)],
    )
    x_other = other_core(layer_in)
    e_other = other_core(enc_states)
    c_other = other_core(cotangent)
    buckets = jnp.concatenate([bucket_table[:1], bucket_table[:0:-1]]).reshape(1, LEN)
    buckets_up = jnp.concatenate([bucket_table[1:], bucket_table[:1]]).reshape(1, LEN)

    at_s = Gather(plan, block_s, direct=True)
    at_c = Gather(plan, block_c, x_other, e_other, c_other)
    at_s.near(block_c)
    at_c.line(*at_s.ready())
    at_s.far()
    at_f1 = Gather(plan, block_f1, *at_s.ready())
    at_c.near(*at_s.ready())
    at_f1.line(*at_c.ready())
    at_c.far()
    at_f2 = Gather(plan, block_f2, *at_c.ready())
    at_f1.near(*at_c.ready())
    part_s, normed_s, qkv, probs_s, mixed_s = self_forward(
        plan, at_s.pieces(), layer_in, after(x_other, *at_f1.ready()), g_self, bias_table.T, buckets, dec_lengths,
        seq_owner,
    )
    part_other = other_core(part_s)
    at_f2.line(part_s)
    at_f1.far(part_s)
    at_f2.near(*at_f1.ready())
    part_c, after_self, normed_c, cq, ckv, probs_c, mixed_c = cross_forward(
        plan, at_c.pieces(), layer_in, x_other, part_s, after(part_other, *at_f2.ready()), g_cross, enc_states,
        e_other, enc_lengths, seq_owner,
    )
    part_other = other_core(part_c)
    at_f2.far()
    after_cross, normed_f, top, out, back, *grads_f1 = feed_first(
        plan, at_f1.pieces(), after_self, part_c, after(part_other, *at_f2.ready()), g_feed, cotangent, c_other,
        dec_lengths, seq_owner,
    )
    sum_f1 = Scatter(plan, grads_f1)
    sums_f, *grads_f2 = feed_second(plan, at_f2.pieces(), normed_f, top, out, back)
    sum_f1.near(sums_f)
    sum_f2 = Scatter(plan, grads_f2)
    total_cross, sums_c, layer_out, gain_feed_row, *grads_c = cross_backward(
        plan, at_c.pieces(), after_cross, top, sums_f, after(other_core(sums_f), *sum_f1.ready()), g_feed, normed_c,
        cq, ckv, probs_c, mixed_c, enc_states, e_other,
    )
    sum_f1.line(sums_c)
    sum_f2.near(sums_c)
    sum_c = Scatter(plan, grads_c)
    total_self, sums_s, grad_states, gain_cross_row, *grads_s = self_backward(
        plan, at_s.pieces(), total_cross, after_self, sums_c, after(other_core(sums_c), *sum_f2.ready()), g_cross,
        normed_s, qkv, probs_s, mixed_s, buckets_up,
    )
    sum_c.near(sums_s)
    sum_s = Scatter(plan, grads_s, *sum_c.ready())
    sums_other = other_core(sums_s)
    sum_f1.last(sums_s)
    grad_in, small = last_norm(
        total_self, layer_in, x_other, sums_s, after(sums_other, *sum_c.ready()), g_self, gain_cross_row,
        gain_feed_row,
    )
    sum_f2.line(sums_s)
    sum_f2.last()
    sum_c.line()
    sum_c.last()
    sum_s.near(small)
    sum_s.direct()
    line_s = sum_s.ready()
    grad_f1 = sum_f1.total(*line_s)
    grad_f2 = sum_f2.total(*line_s)
    grad_c = sum_c.total(*line_s)
    grad_s = sum_s.total()
    small = sum_everywhere(plan, small, line_s)
    small = jnp.concatenate([small[:4], small[4:]], axis=1)
    table_grad = small[3, : H * NB].reshape(H, NB).T

    def columns(block, number, size):
        return block[:, number * size : (number + 1) * size]

    def feed(number):
        return jnp.concatenate([columns(g, number, units) for g in (grad_f1, grad_f2)], axis=1)

    return (
        layer_out,
        grad_in,
        grad_states,
        small[0],
        small[1],
        small[2],
        table_grad,
        columns(grad_s, 0, width),
        columns(grad_s, 1, width),
        columns(grad_s, 2, width),
        columns(grad_s, 3, width).T,
        columns(grad_c, 0, width),
        columns(grad_c, 1, width),
        columns(grad_c, 2, width),
        columns(grad_c, 3, width).T,
        feed(0),
        feed(1),
        feed(2).T,
    )


def solution(mesh):
    rows = P(("dp", "tensor"), None)
    into, out = P("dp", "tensor"), P("tensor", "dp")
    weights = (into, into, into, out, into, into, into, out, into, into, out)
    in_specs = (rows, rows, rows, P(), P(), P(), P(), *weights, P(), P(), P(), P())
    out_specs = (rows, rows, rows, P(), P(), P(), P(), *weights)
    return jax.shard_map(
        functools.partial(shards, mesh), mesh=mesh, in_specs=in_specs, out_specs=out_specs, check_vma=False
    )
```
